256 devices in a mesh: blk: 16 (over x_lo, z), beam: 2 (over x_hi), head: 8 (over y, core).
Axes of the slice: x: 4 (x_hi: 2, x_lo: 2; x = x_hi * 2 + x_lo), y: 4, z: 8, core: 2. Of those that a mesh axis runs over, the one named last changes fastest.
Arguments:
- hidden_in: float32 [2, 512, 4096], P(None, 'beam', 'blk'), may hold values from -41 to 41
- norm_gains: float32 [2, 4096], P(None, 'blk'), may hold values from 0.1 to 1.9
- w_qkv: bfloat16 [4096, 3, 4096], P('blk', None, 'head'), may hold values from -0.09375 to 0.09375
- w_self_out: bfloat16 [4096, 4096], P('head', 'blk'), may hold values from -0.09375 to 0.09375
- w_cross_q: bfloat16 [4096, 4096], P('blk', 'head'), may hold values from -0.09375 to 0.09375
- w_cross_out: bfloat16 [4096, 4096], P('head', 'blk'), may hold values from -0.09375 to 0.09375
- pos_bias: float32 [64, 8], P('head'), may hold values from -4 to 4
- self_cache: bfloat16 [2, 2, 256, 6, 4096], P(None, 'beam', 'blk', None, 'head'), may hold values from -300 to 300
- memory: bfloat16 [2, 2048, 4096], P(None, 'blk', 'head'), may hold values from -300 to 300
- parents: int32 [2, 512], replicated, may hold values from 0 to 511, as said below
Outputs:
- hidden_out: float32 [2, 512, 4096], P(None, 'beam', 'blk')
- cache_out: bfloat16 [2, 2, 256, 8, 4096], P(None, 'beam', 'blk', None, 'head')
The draws below stay inside these ranges and needn't reach their ends.
Inputs may be any that keep to these rules, and one draw needn't show every extreme that they name: In every step each aligned block of 16 rows takes at most 2 of its parents from any one aligned block of 16 rows, and exactly 2 from at least one.
All inputs are finite; a program needn't handle non-finite values.
Results may differ from the reference program's by a relative error of at most 0.022.
Values may be sent and summed in bfloat16 or wider, within the bound.
A program may use at most 128 MiB of HBM per device.

```python
import jax
import jax.numpy as jnp
from jax import lax

D = 4096
HEADS = 64
HEAD_DIM = 64
INNER = 4096
ROWS_DEV = 16
GROUP_ROWS = 256
ROWS = 512
PREV = 6
STEPS = 2
LEN = 8
ENC = 2048
N_BEAM = 2


def spread_scales(seed_key, full_shape):
    return jnp.exp(jax.random.uniform(seed_key, full_shape, jnp.float32, 0.0, 2.302585)) * 0.316228


def draw_hidden_in(key, part):
    subkeys = jax.random.split(key, 3)
    row_scale = spread_scales(subkeys[1], (STEPS, ROWS, 1))
    col_scale = spread_scales(subkeys[2], (1, 1, D))
    baseline = jnp.clip(jax.random.normal(subkeys[0], (STEPS, ROWS, D), jnp.float32), -4.0, 4.0)
    return baseline * row_scale * col_scale


def attention_table(seed_key, leading, length, key_scale, value_scale):
    subkeys = jax.random.split(seed_key, 1)
    full_shape = (2,) + leading + (length, INNER)
    normal_raw = jnp.clip(jax.random.normal(subkeys[0], full_shape, jnp.float32), -4.0, 4.0)
    key_part = normal_raw[0] * key_scale
    value_part = normal_raw[1] * value_scale
    return jnp.stack([key_part, value_part]).astype(jnp.bfloat16)


def draw_self_cache(key, part):
    return attention_table(key, (ROWS // GROUP_ROWS, GROUP_ROWS), PREV, 2.0, 1.5)


def draw_memory(key, part):
    return attention_table(key, (), ENC, 2.5, 2.0)


def draw_parents(key, part):
    subkeys = jax.random.split(key, 5)
    groups = ROWS // ROWS_DEV
    capacity = max(2, -(-ROWS_DEV // groups))
    lowest = -(-ROWS_DEV // capacity)
    highest = min(groups, ROWS_DEV - capacity + 1)
    favour = jax.random.randint(subkeys[0], (STEPS, 1, groups), 0, 4)
    ranking = jax.random.randint(subkeys[1], (STEPS, groups, groups), 0, 16) + favour * favour * 8
    ranking = ranking * groups + jnp.arange(groups, dtype=jnp.int32)
    ranked = jnp.argsort(-ranking, axis=2)
    distinct = lowest + jax.random.randint(subkeys[2], (STEPS, groups, 1), 0, highest - lowest + 1)
    entry = jnp.arange(ROWS_DEV, dtype=jnp.int32)[None, None, :]
    chosen = jnp.where(entry < capacity, 0, 1 + (entry - capacity) % (distinct - 1))
    sources = jnp.take_along_axis(ranked, chosen, axis=2)
    shuffle_rank = jax.random.randint(subkeys[3], (STEPS, groups, ROWS_DEV), 0, 1 << 20) * ROWS_DEV + entry
    shuffled = jnp.argsort(shuffle_rank, axis=2)
    sources = jnp.take_along_axis(sources, shuffled, axis=2)
    local_rows = jax.random.randint(subkeys[4], (STEPS, groups, ROWS_DEV), 0, ROWS_DEV)
    return (sources * ROWS_DEV + local_rows).reshape(STEPS, ROWS).astype(jnp.int32)


def levels(own_key, extent, cuts, low, largest):
    gain = 1.0
    for dim, shards_of in cuts:
        heights = jax.random.uniform(jax.random.fold_in(jax.random.fold_in(own_key, 6), dim), (shards_of,), jnp.float32, low / len(cuts), largest / len(cuts))
        gain = gain * jnp.repeat(jnp.exp(heights), extent[dim] // shards_of).reshape((-1,) + (1,) * (len(extent) - 1 - dim))
    return gain


def centred(stream_key, dims, spread, bound, cuts=(), kind=jnp.bfloat16):
    factor_of = levels(stream_key, dims, cuts, -0.22, 0.18) if cuts else 1.0
    entries = jax.random.normal(stream_key, dims, jnp.float32) * spread * factor_of
    return jnp.minimum(jnp.maximum(entries, -bound), bound).astype(kind)


def setup_inputs(seed: int = 0) -> dict:
    splits = jax.random.split(jax.random.key(seed), 11)
    hidden_in = draw_hidden_in(jax.random.fold_in(splits[10], 71), 0)
    norm_gains = jnp.clip(1.0 + 0.18 * jax.random.normal(splits[1], (2, D), jnp.float32), 0.1, 1.9)
    w_qkv = centred(splits[2], (D, 3, INNER), D ** -0.5, 0.09375, ((0, 16), (2, 8)))
    w_self_out = centred(splits[3], (INNER, D), INNER ** -0.5, 0.09375, ((0, 8), (1, 16)))
    w_cross_q = centred(splits[4], (D, INNER), D ** -0.5, 0.09375, ((0, 16), (1, 8)))
    w_cross_out = centred(splits[5], (INNER, D), INNER ** -0.5, 0.09375, ((0, 8), (1, 16)))
    pos_bias = centred(splits[6], (HEADS, LEN), 1.0, 4.0, ((0, 8),), jnp.float32)
    self_cache = draw_self_cache(jax.random.fold_in(splits[10], 71), 0)
    memory = draw_memory(jax.random.fold_in(splits[10], 71), 0)
    parents = draw_parents(jax.random.fold_in(splits[10], 71), 0)
    return dict(hidden_in=hidden_in, norm_gains=norm_gains, w_qkv=w_qkv, w_self_out=w_self_out, w_cross_q=w_cross_q, w_cross_out=w_cross_out, pos_bias=pos_bias, self_cache=self_cache, memory=memory, parents=parents)


EPS = 1e-06

def inverse_rms(states):
    return lax.rsqrt(lax.optimization_barrier(jnp.mean(states * states, axis=1, keepdims=True)) + EPS)

def self_attend(queries, grown_cache, position_bias):
    length = grown_cache.shape[2]
    split_queries = queries.reshape(ROWS, HEADS, HEAD_DIM).astype(jnp.float32)
    key_part = grown_cache[0].reshape(ROWS, length, HEADS, HEAD_DIM).astype(jnp.float32)
    value_part = grown_cache[1].reshape(ROWS, length, HEADS, HEAD_DIM).astype(jnp.float32)
    scores = jnp.einsum('rhd,rjhd->rhj', split_queries, key_part) * HEAD_DIM ** (-0.5) + position_bias[None]
    maxima = lax.optimization_barrier(jnp.max(scores, axis=2, keepdims=True))
    weights = jnp.exp(scores - maxima)
    totals = lax.optimization_barrier(jnp.sum(weights, axis=2))
    rounded = lax.optimization_barrier(weights.astype(jnp.bfloat16)).astype(jnp.float32)
    mixed = jnp.einsum('rhj,rjhd->rhd', rounded, value_part) / totals[:, :, None]
    return mixed.reshape(ROWS, INNER).astype(jnp.bfloat16)

def cross_attend(queries, memory):

    def one_head(head_index):
        first_col = head_index * HEAD_DIM
        head_queries = lax.dynamic_slice_in_dim(queries, first_col, HEAD_DIM, 1)
        head_memory = lax.dynamic_slice_in_dim(memory, first_col, HEAD_DIM, 2)
        scores = jnp.dot(head_queries, head_memory[0].T, preferred_element_type=jnp.float32) * HEAD_DIM ** (-0.5)
        maxima = lax.optimization_barrier(jnp.max(scores, axis=1, keepdims=True))
        weights = jnp.exp(scores - maxima)
        totals = lax.optimization_barrier(jnp.sum(weights, axis=1))
        mixed = jnp.dot(weights.astype(jnp.bfloat16), head_memory[1], preferred_element_type=jnp.float32)
        return mixed / totals[:, None]
    stacked = lax.map(one_head, jnp.arange(HEADS, dtype=jnp.int32))
    return jnp.transpose(stacked, (1, 0, 2)).reshape(ROWS, INNER).astype(jnp.bfloat16)

def reference(hidden_in, norm_gains, w_qkv, w_self_out, w_cross_q, w_cross_out, pos_bias, self_cache, memory, parents):
    cache = self_cache.reshape(2, ROWS, PREV, INNER)
    united_qkv = w_qkv.reshape(D, 3 * INNER)
    outputs = []
    for step_index in range(STEPS):
        states = hidden_in[step_index]
        reordered = jnp.take(cache, parents[step_index], axis=1)
        normed = (states * norm_gains[0]).astype(jnp.bfloat16)
        qkv = (jnp.dot(normed, united_qkv, preferred_element_type=jnp.float32) * inverse_rms(states)).astype(jnp.bfloat16)
        queries = qkv[:, :INNER]
        fresh_entry = jnp.stack([qkv[:, INNER:2 * INNER], qkv[:, 2 * INNER:]])[:, :, None]
        grown_cache = jnp.concatenate([reordered, fresh_entry], axis=2)
        length = PREV + step_index + 1
        position_bias = jnp.flip(pos_bias[:, :length], axis=1)
        self_mixed = self_attend(queries, grown_cache, position_bias)
        middle = states + jnp.dot(self_mixed, w_self_out, preferred_element_type=jnp.float32)
        normed_cross = (middle * norm_gains[1]).astype(jnp.bfloat16)
        cross_query = (jnp.dot(normed_cross, w_cross_q, preferred_element_type=jnp.float32) * inverse_rms(middle)).astype(jnp.bfloat16)
        cross_mixed = cross_attend(cross_query, memory)
        outputs.append(middle + jnp.dot(cross_mixed, w_cross_out, preferred_element_type=jnp.float32))
        cache = grown_cache
    return (jnp.stack(outputs), cache.reshape(2, N_BEAM, GROUP_ROWS, LEN, INNER))
```

```python
import jax
import jax.numpy as jnp
from jax import lax
from jax.experimental import pallas as pl
from jax.experimental.pallas import tpu as pltpu
from jax.sharding import PartitionSpec as P

D = 4096
EPS = 1e-06
MESH = pl.DeviceIdType.MESH
F32, BF16 = jnp.float32, jnp.bfloat16
NZ, NX, NB = 8, 2, 2
NBLK, NALL = NZ * NX, NZ * NX * NB
NY, NC = 4, 2
RB = 16
BLK = 2 * RB
ROWS = NBLK * BLK
HALF = ROWS // 2
INNER = 512
COLS = 256
PREV = 6
CP = 2 * PREV * 2
KP = 8
LANES = 128
SLOTS = 2


def dot(a, b):
    return jnp.dot(a, b, preferred_element_type=F32)


def dot_t(a, b):
    return lax.dot_general(a, b, (((1,), (1,)), ((), ())), preferred_element_type=F32)


def iota(shape, dim):
    return lax.broadcasted_iota(jnp.int32, shape, dim)


def split3(x):
    high = x.astype(BF16).astype(F32)
    middle = (x - high).astype(BF16).astype(F32)
    return high, middle, x - high - middle


def encode(x):
    high, middle, low = split3(x)
    place = iota(x.shape, 1) & 15
    return jnp.where(place < 4, high, jnp.where(place < 8, middle, low)).astype(BF16)


def part_weight(place, lanes):
    return jnp.where(place < 8, 4.0 / lanes, 2.0 / lanes)


def decode_row():
    lane = iota((LANES, LANES), 0)
    return part_weight(lane & 15, LANES).astype(BF16)


def decode_heads():
    lane, col = iota((LANES, INNER), 0), iota((LANES, INNER), 1)
    same = ((lane >> 6) == ((col >> 6) & 1)) & (((lane >> 4) & 3) == (col >> 7))
    return jnp.where(same, part_weight(lane & 15, 16), 0.0).astype(BF16)


def spread_matrix(chosen, pieces, rows, cols):
    rowf = (iota((rows, cols), 0).astype(F32) + 0.5) * (1.0 / pieces)
    piece = (rowf - jnp.floor(rowf)) * pieces
    col_piece = (iota((rows, cols), 1) >> 4).astype(F32)
    keep = jnp.abs(piece - 0.5 - col_piece) < 0.25
    slot_row = iota((rows, NALL * SLOTS), 0)
    slot = iota((rows, NALL * SLOTS), 1) * pieces
    expand = jnp.where((slot_row >= slot) & (slot_row < slot + pieces), 1.0, 0.0).astype(BF16)
    repeat = jnp.where((iota((RB, cols), 1) & 15) == iota((RB, cols), 0), 1.0, 0.0).astype(BF16)
    wide = dot(chosen, repeat).astype(BF16)
    return jnp.where(keep, dot(expand, wide), 0.0).astype(BF16)


def gather_matrix(chosen, pieces, rows, cols):
    colf = (iota((rows, cols), 1).astype(F32) + 0.5) * (1.0 / pieces)
    piece = (colf - jnp.floor(colf)) * pieces
    row_piece = (iota((rows, cols), 0) >> 4).astype(F32)
    keep = jnp.abs(piece - 0.5 - row_piece) < 0.25
    slot_col = iota((NALL * SLOTS, cols), 1)
    slot = iota((NALL * SLOTS, cols), 0) * pieces
    expand = jnp.where((slot_col >= slot) & (slot_col < slot + pieces), 1.0, 0.0).astype(BF16)
    repeat = jnp.where((iota((rows, RB), 0) & 15) == iota((rows, RB), 1), 1.0, 0.0).astype(BF16)
    tall = dot(repeat, chosen).astype(BF16)
    return jnp.where(keep, dot(tall, expand), 0.0).astype(BF16)


def kernel(
    hidden, gains, wqkv, wso, wcq, wco, bias, cache, memory, send_pick, recv_pick,
    out, cache_out,
    hid, xs1, xr1, zs1, zr1, own1, xs2, xr2, zs2, zr2, own2, xs3, xr3, zs3, zr3, own3, lse3,
    hop_send, hop_recv, kv_send, kv_recv, att, query, mixed,
    core_s, core_r, ys, yr, delta, core_s2, core_r2, ys2, yr2, delta2,
    sem_xs, sem_xr, sem_zs, sem_zr, sem_hs, sem_hr, sem_ks, sem_kr, sem_gs, sem_gr, sem_fs, sem_fr,
    sem_cs, sem_cr, sem_ys, sem_yr, sem_ds, sem_dr, sem_es, sem_er,
):
    blk, beam, head = lax.axis_index("blk"), lax.axis_index("beam"), lax.axis_index("head")
    x, z = blk // NZ, lax.rem(blk, NZ)
    y, core = head // NC, lax.rem(head, NC)

    def block_at(dx, dz):
        return (x if dx == 0 else 1 - x) * NZ + lax.rem(z + dz, NZ)

    def z_peer(dz):
        return {"blk": block_at(0, dz)}

    x_peer = {"blk": block_at(1, 0)}

    def all_peer(o):
        where = {"blk": block_at((o // NZ) % NX, o % NZ)}
        if o >= NBLK:
            where["beam"] = 1 - beam
        return where

    core_peer = {"head": y * NC + 1 - core}

    def y_peer(dy):
        return {"head": lax.rem(y + dy, NY) * NC + core}

    def remote(src, dst, send, recv, peer):
        return pltpu.make_async_remote_copy(
            src, dst, send, recv, device_id=peer, device_id_type=MESH
        )

    barrier = pltpu.get_barrier_semaphore()
    peers = [all_peer(o) for o in range(1, NALL)]
    peers += [core_peer] + [y_peer(dy) for dy in range(1, NY)]
    for peer in peers:
        pl.semaphore_signal(barrier, inc=1, device_id=peer, device_id_type=MESH)
    pl.semaphore_wait(barrier, len(peers))

    pending = []

    def x_send(phase, xs, xr):
        for dz in range(NZ):
            copy = remote(xs.at[dz], xr.at[dz], sem_xs.at[phase, dz], sem_xr.at[phase, dz], x_peer)
            copy.start()
            pending.append(copy)

    def x_wait(phase, xs, xr, dz):
        remote(xs.at[dz], xr.at[dz], sem_xs.at[phase, dz], sem_xr.at[phase, dz], x_peer).wait_recv()

    def z_copy(phase, zs, zr, dz):
        return remote(
            zs.at[dz - 1], zr.at[dz - 1], sem_zs.at[phase, dz - 1], sem_zr.at[phase, dz - 1], z_peer(dz)
        )

    far_first = (4, 3, 5, 2, 6, 1, 7)

    def scatter_sums(phase, width, xs, xr, zs, zr, own):
        def joined(dz):
            x_wait(phase, xs, xr, dz)
            rows = pl.ds(dz * BLK, BLK)
            arrived = xr[dz]
            total = own[rows, :width] + arrived[:, :width].astype(F32)
            squares = own[rows, width:] + dot(arrived[:, width:], decode_row())
            return total, squares

        for dz in far_first:
            total, squares = joined(dz)
            zs[dz - 1, :, :width] = total.astype(BF16)
            zs[dz - 1, :, width:] = encode(squares)
            copy = z_copy(phase, zs, zr, dz)
            copy.start()
            pending.append(copy)
        total, squares = joined(0)
        for dz in far_first[::-1]:
            z_copy(phase, zs, zr, dz).wait_recv()
            arrived = zr[dz - 1]
            total += arrived[:, :width].astype(F32)
            squares += dot(arrived[:, width:], decode_row())
        return total, lax.rsqrt(squares[:, :1] / D + EPS)

    def partial_products(states, gain, weight, width, xs, xr, phase, own):
        normed = (states * gain).astype(BF16)
        squares = jnp.sum(states * states, axis=1, keepdims=True)
        squares = jnp.broadcast_to(squares, (ROWS, LANES))
        far = dot(normed[HALF:], weight).astype(BF16)
        code = encode(squares[HALF:])
        for dz in range(NZ):
            xs[dz, :, :width] = far[dz * BLK : (dz + 1) * BLK]
            xs[dz, :, width:] = code[dz * BLK : (dz + 1) * BLK]
        x_send(phase, xs, xr)
        own[:, :width] = dot(normed[:HALF], weight)
        own[:, width:] = squares[:HALF]

    def gather_rows(phase, blocks):
        def copy_z(dz):
            back = (NZ - dz) % NZ
            return remote(
                blocks.at[0], blocks.at[back], sem_gs.at[phase, dz], sem_gr.at[phase, back], z_peer(dz)
            )

        def copy_x(dz):
            return remote(
                blocks.at[dz], blocks.at[NZ + dz], sem_fs.at[phase, dz], sem_fr.at[phase, dz], x_peer
            )

        for dz in far_first:
            copy_z(dz).start()
        copy_x(0).start()
        for dz in far_first[::-1]:
            remote(
                blocks.at[0], blocks.at[dz], sem_gs.at[phase, dz], sem_gr.at[phase, dz], z_peer(dz)
            ).wait_recv()
            copy_x(dz).start()
        for dz in range(NZ):
            copy_x(dz).wait()
        for dz in far_first:
            copy_z(dz).wait_send()
        return blocks[...].reshape(ROWS, INNER)

    def head_sums(phase, product, core_s, core_r, ys, yr, delta):
        mine, other = pl.ds(pl.multiple_of(core * HALF, HALF), HALF), 1 - core
        own2[:, :COLS] = product[:HALF]
        own2[:, COLS:INNER] = product[HALF:]
        first, second = own2[:, :COLS], own2[:, COLS:INNER]
        is_first = core == 0
        core_s[...] = jnp.where(is_first, second, first).astype(BF16)
        copy = remote(core_s, core_r, sem_cs.at[phase], sem_cr.at[phase], core_peer)
        copy.start()
        kept = jnp.where(is_first, first, second)
        copy.wait()
        kept = (kept + core_r[...].astype(F32)).reshape(NY, HALF // NY, COLS)
        own3[:, :COLS] = kept.reshape(HALF, COLS)
        quarter = HALF // NY

        def rows_of(dy):
            return pl.ds(pl.multiple_of(lax.rem(y + dy, NY) * quarter, quarter), quarter)

        order = (2, 1, 3)
        for dy in order:
            ys[dy - 1] = own3[rows_of(dy), :COLS].astype(BF16)
            remote(
                ys.at[dy - 1], yr.at[dy - 1], sem_ys.at[phase, dy - 1], sem_yr.at[phase, dy - 1], y_peer(dy)
            ).start()
        total = own3[rows_of(0), :COLS]
        for dy in (1, 3, 2):
            remote(
                ys.at[dy - 1], yr.at[dy - 1], sem_ys.at[phase, dy - 1], sem_yr.at[phase, dy - 1], y_peer(dy)
            ).wait()
            total += yr[dy - 1].astype(F32)
        delta[0, 0] = total.astype(BF16)

        def copy_y(dy):
            back = (NY - dy) % NY
            return remote(
                delta.at[0, 0], delta.at[0, back], sem_ds.at[phase, dy], sem_dr.at[phase, back], y_peer(dy)
            )

        def copy_c(dy):
            return remote(
                delta.at[0, dy], delta.at[1, dy], sem_es.at[phase, dy], sem_er.at[phase, dy], core_peer
            )

        for dy in order:
            copy_y(dy).start()
        copy_c(0).start()
        for dy in (1, 3, 2):
            remote(
                delta.at[0, 0], delta.at[0, dy], sem_ds.at[phase, dy], sem_dr.at[phase, dy], y_peer(dy)
            ).wait_recv()
            copy_c(dy).start()
        for dy in range(NY):
            copy_c(dy).wait()
        for dy in order:
            copy_y(dy).wait_send()
        for part in range(2):
            half = core if part == 0 else other
            for dy in range(NY):
                start = half * HALF + lax.rem(y + dy, NY) * quarter
                rows = pl.ds(pl.multiple_of(start, quarter), quarter)
                hid[rows, :] += delta[part, dy].astype(F32)

    for o in range(NBLK):
        first = pl.multiple_of(block_at(o // NZ, o % NZ) * RB, RB)
        for t in range(2):
            hid[o * BLK + t * RB : o * BLK + (t + 1) * RB, :] = hidden[t, pl.ds(first, RB), :]
    width1 = 3 * INNER
    partial_products(hid[...], gains[0:1, :], wqkv[...], width1, xs1, xr1, 0, own1)

    def hop_start(step, rows):
        spread = spread_matrix(send_pick[step], CP, NALL * SLOTS * CP, RB * CP)
        hop_send[step] = dot(spread, rows).astype(BF16).reshape(NALL, SLOTS * CP, COLS)
        hop_recv[step, 0] = hop_send[step, 0]
        for o in range(1, NALL):
            copy = remote(
                hop_send.at[step, o], hop_recv.at[step, o], sem_hs.at[step, o], sem_hr.at[step, o], all_peer(o)
            )
            copy.start()
            pending.append(copy)

    def hop_end(step):
        pick = gather_matrix(recv_pick[step], CP, RB * CP, NALL * SLOTS * CP)
        for o in range(1, NALL):
            remote(
                hop_send.at[step, o], hop_recv.at[step, o], sem_hs.at[step, o], sem_hr.at[step, o], all_peer(o)
            ).wait_recv()
        return dot(pick, hop_recv[step].reshape(NALL * SLOTS * CP, COLS)).astype(BF16)

    hop_start(0, cache[...])
    total, scale = scatter_sums(0, width1, xs1, xr1, zs1, zr1, own1)
    qkv = (total * scale).astype(BF16)
    held0 = hop_end(0)
    hop_start(1, held0)

    fresh = qkv[:RB, INNER:]
    stacked = jnp.concatenate([fresh[:, p * LANES : (p + 1) * LANES] for p in range(KP)], axis=0)
    spread = spread_matrix(send_pick[1], KP, NALL * SLOTS * KP, RB * KP)
    kv_send[...] = dot(spread, stacked).astype(BF16).reshape(NALL, SLOTS * KP, LANES)
    kv_recv[0] = kv_send[0]

    def kv_copy(o):
        return remote(kv_send.at[o], kv_recv.at[o], sem_ks.at[o], sem_kr.at[o], all_peer(o))

    for o in range(1, NALL):
        copy = kv_copy(o)
        copy.start()
        pending.append(copy)
    held1 = hop_end(1)
    pick = gather_matrix(recv_pick[1], KP, RB * KP, NALL * SLOTS * KP)
    for o in range(1, NALL):
        kv_copy(o).wait_recv()
    moved = dot(pick, kv_recv[...].reshape(NALL * SLOTS * KP, LANES)).astype(BF16)

    def entry(kv, rows):
        first = kv * KP // 2
        return jnp.concatenate(
            [rows[(first + p) * RB : (first + p + 1) * RB] for p in range(KP // 2)], axis=1
        )

    def position(held, kv, pos):
        first = (kv * PREV + pos) * 2
        return jnp.concatenate([held[(first + c) * RB : (first + c + 1) * RB] for c in range(2)], axis=1)

    own_kv = [
        [qkv[t * RB : (t + 1) * RB, (1 + kv) * INNER : (2 + kv) * INNER] for kv in range(2)]
        for t in range(2)
    ]
    grown = []
    for t, held in enumerate((held0, held1)):
        sides = []
        for kv in range(2):
            side = [position(held, kv, pos) for pos in range(PREV)]
            if t == 1:
                side.append(entry(kv, moved))
            side.append(own_kv[t][kv])
            sides.append(side)
        grown.append(sides)
    for kv in range(2):
        for pos in range(PREV + 2):
            cache_out[kv, pos] = grown[1][kv][pos]

    same_head = (
        (iota((INNER, INNER), 0) >> 6) == (iota((INNER, INNER), 1) >> 6)
    )
    ones = jnp.where(same_head, 1.0, 0.0).astype(BF16)
    for t in range(2):
        keys, values = grown[t]
        q = qkv[t * RB : (t + 1) * RB, :INNER].astype(F32) * 0.125
        products = jnp.concatenate([q * k.astype(F32) for k in keys], axis=0)
        high = products.astype(BF16)
        low = (products - high.astype(F32)).astype(BF16)
        sums = dot(high, ones) + dot(low, ones)
        last = PREV + t
        scores = [
            sums[j * RB : (j + 1) * RB] + bias[last - j : last - j + 1, :] for j in range(last + 1)
        ]
        peak = scores[0]
        for s in scores[1:]:
            peak = jnp.maximum(peak, s)
        weights = [jnp.exp(s - peak) for s in scores]
        whole, acc = weights[0], weights[0].astype(BF16).astype(F32) * values[0].astype(F32)
        for w, v in zip(weights[1:], values[1:]):
            whole += w
            acc += w.astype(BF16).astype(F32) * v.astype(F32)
        att[0, t * RB : (t + 1) * RB, :] = (acc / whole).astype(BF16)
    head_sums(0, dot(gather_rows(0, att), wso[...]), core_s, core_r, ys, yr, delta)

    partial_products(hid[...], gains[1:2, :], wcq[...], INNER, xs2, xr2, 1, own2)
    total, scale = scatter_sums(1, INNER, xs2, xr2, zs2, zr2, own2)
    query[0] = ((total * scale).astype(BF16).astype(F32) * 0.125).astype(BF16)
    queries = gather_rows(1, query)
    tokens = memory.shape[1]
    low_lane = iota((tokens, LANES), 1) < 64
    accs, lses = [], []
    for p in range(INNER // LANES):
        cols = slice(p * LANES, (p + 1) * LANES)
        k, v = memory[0, :, cols].astype(F32), memory[1, :, cols].astype(F32)
        k2 = jnp.concatenate([jnp.where(low_lane, k, 0.0), jnp.where(low_lane, 0.0, k)], axis=0)
        one = jnp.where(low_lane, 1.0, 0.0)
        v2 = jnp.concatenate(
            [
                jnp.concatenate([jnp.where(low_lane, v, 0.0), one], axis=1),
                jnp.concatenate([jnp.where(low_lane, 0.0, v), 1.0 - one], axis=1),
            ],
            axis=0,
        )
        scores = dot_t(queries[:, cols], k2.astype(BF16))
        peak0 = jnp.max(scores[:, :tokens], axis=1, keepdims=True)
        peak1 = jnp.max(scores[:, tokens:], axis=1, keepdims=True)
        weights = jnp.concatenate(
            [jnp.exp(scores[:, :tokens] - peak0), jnp.exp(scores[:, tokens:] - peak1)], axis=1
        )
        both = dot(weights.astype(BF16), v2.astype(BF16))
        low_out = iota((ROWS, LANES), 1) < 64
        lse = jnp.where(low_out, peak0, peak1) + jnp.log(both[:, LANES:])
        acc = both[:, :LANES] / both[:, LANES:]
        own3[:, cols] = acc[:HALF]
        lse3[:, cols] = lse[:HALF]
        far = acc[HALF:].astype(BF16)
        for dz in range(NZ):
            xs3[dz, :, cols] = far[dz * BLK : (dz + 1) * BLK]
        accs.append(None)
        lses.append(lse[HALF:])
    group = (iota((HALF, LANES), 1) >> 4) & 3
    code = jnp.where(group == 0, lses[0], jnp.where(group == 1, lses[1], jnp.where(group == 2, lses[2], lses[3])))
    code = encode(code)
    for dz in range(NZ):
        xs3[dz, :, INNER:] = code[dz * BLK : (dz + 1) * BLK]
    x_send(2, xs3, xr3)

    spread_heads = decode_heads()

    def joined(dz):
        x_wait(2, xs3, xr3, dz)
        rows = pl.ds(dz * BLK, BLK)
        arrived = xr3[dz]
        other = dot(arrived[:, INNER:], spread_heads)
        mine = lse3[rows, :]
        peak = jnp.maximum(mine, other)
        w_mine, w_other = jnp.exp(mine - peak), jnp.exp(other - peak)
        whole = w_mine + w_other
        acc = own3[rows, :INNER] * w_mine + arrived[:, :INNER].astype(F32) * w_other
        return acc / whole, peak + jnp.log(whole)

    for dz in far_first:
        acc, lse = joined(dz)
        zs3[dz - 1, :, :INNER] = acc.astype(BF16)
        place = (iota((BLK, LANES), 1) >> 4) & 3
        four = [lse[:, p * LANES : (p + 1) * LANES] for p in range(4)]
        picked = jnp.where(place == 0, four[0], jnp.where(place == 1, four[1], jnp.where(place == 2, four[2], four[3])))
        zs3[dz - 1, :, INNER:] = encode(picked)
        copy = z_copy(2, zs3, zr3, dz)
        copy.start()
        pending.append(copy)
    acc, peak = joined(0)
    parts = [(acc, peak)]
    for dz in far_first[::-1]:
        z_copy(2, zs3, zr3, dz).wait_recv()
        arrived = zr3[dz - 1]
        parts.append((arrived[:, :INNER].astype(F32), dot(arrived[:, INNER:], spread_heads)))
        peak = jnp.maximum(peak, parts[-1][1])
    weights = [jnp.exp(l - peak) for _, l in parts]
    acc, whole = parts[0][0] * weights[0], weights[0]
    for (a, _), w in zip(parts[1:], weights[1:]):
        acc += a * w
        whole += w
    mixed[0] = (acc / whole).astype(BF16)
    head_sums(1, dot(gather_rows(2, mixed), wco[...]), core_s2, core_r2, ys2, yr2, delta2)

    for o in range(NBLK):
        first = pl.multiple_of(block_at(o // NZ, o % NZ) * RB, RB)
        for t in range(2):
            out[t, pl.ds(first, RB), :] = hid[o * BLK + t * RB : o * BLK + (t + 1) * RB, :]
    for copy in pending:
        copy.wait_send()


def picks(parent_list):
    blk, beam = lax.axis_index("blk"), lax.axis_index("beam")
    x, z = blk // NZ, blk % NZ
    me = beam * NBLK + blk
    o = jnp.arange(NALL, dtype=jnp.int32)
    at_offset = (beam ^ o // NBLK) * NBLK + (x ^ (o // NZ) % NX) * NZ + (z + o % NZ) % NZ
    placed = at_offset[:, None] == jnp.arange(NALL, dtype=jnp.int32)
    blocks = jnp.sum(jnp.where(placed[:, :, None], parent_list.reshape(1, NALL, RB), 0), axis=1)
    source, local = blocks // RB, blocks % RB
    order = jnp.arange(RB, dtype=jnp.int32)
    same = source[:, :, None] == source[:, None, :]
    slot = jnp.sum((same & (order[None, :] < order[:, None])[None]).astype(jnp.int32), axis=2)
    entries = (source == me)[:, None, :] & (slot[:, None, :] == jnp.arange(SLOTS, dtype=jnp.int32)[None, :, None])
    chosen = entries[:, :, :, None] & (local[:, None, :, None] == order)
    send = jnp.any(chosen, axis=2).reshape(NALL * SLOTS, RB)
    own_source = source[0]
    sb, sx, sz = own_source // NBLK, (own_source // NZ) % NX, own_source % NZ
    offset = (sb ^ beam) * NBLK + (sx ^ x) * NZ + (z - sz + NZ) % NZ
    recv = (offset * SLOTS + slot[0])[:, None] == jnp.arange(NALL * SLOTS, dtype=jnp.int32)
    return send.astype(BF16), recv.astype(BF16)


def body(
    hidden_in, norm_gains, w_qkv, w_self_out, w_cross_q, w_cross_out, pos_bias, self_cache, memory, parents
):
    steps = [picks(parents[t]) for t in range(2)]
    send_pick = jnp.stack([s for s, _ in steps])
    recv_pick = jnp.stack([r for _, r in steps])
    bias = jnp.repeat(pos_bias.T, 64, axis=1)
    cache = self_cache[:, 0].reshape(2, RB, PREV, 2, COLS).transpose(0, 2, 3, 1, 4).reshape(CP * RB, COLS)
    dma = pltpu.SemaphoreType.DMA

    def exchange(width):
        wide = width + LANES
        return [
            pltpu.VMEM((NZ, BLK, wide), BF16),
            pltpu.VMEM((NZ, BLK, wide), BF16),
            pltpu.VMEM((NZ - 1, BLK, wide), BF16),
            pltpu.VMEM((NZ - 1, BLK, wide), BF16),
            pltpu.VMEM((HALF, wide), F32),
        ]

    head_buffers = [
        pltpu.VMEM((HALF, COLS), BF16),
        pltpu.VMEM((HALF, COLS), BF16),
        pltpu.VMEM((NY - 1, HALF // NY, COLS), BF16),
        pltpu.VMEM((NY - 1, HALF // NY, COLS), BF16),
        pltpu.VMEM((2, NY, HALF // NY, COLS), BF16),
    ]
    in_vmem = pl.BlockSpec(memory_space=pltpu.VMEM)
    hidden_out, cache_rows = pl.pallas_call(
        kernel,
        out_shape=(
            jax.ShapeDtypeStruct(hidden_in.shape, F32),
            jax.ShapeDtypeStruct((2, PREV + 2, RB, INNER), BF16),
        ),
        in_specs=[in_vmem] * 11,
        out_specs=(in_vmem, in_vmem),
        scratch_shapes=[
            pltpu.VMEM((ROWS, COLS), F32),
            *exchange(3 * INNER),
            *exchange(INNER),
            *exchange(INNER),
            pltpu.VMEM((HALF, INNER), F32),
            pltpu.VMEM((2, NALL, SLOTS * CP, COLS), BF16),
            pltpu.VMEM((2, NALL, SLOTS * CP, COLS), BF16),
            pltpu.VMEM((NALL, SLOTS * KP, LANES), BF16),
            pltpu.VMEM((NALL, SLOTS * KP, LANES), BF16),
            *[pltpu.VMEM((NBLK, BLK, INNER), BF16)] * 3,
            *head_buffers,
            *head_buffers,
            dma((3, NZ)), dma((3, NZ)), dma((3, NZ - 1)), dma((3, NZ - 1)),
            dma((2, NALL)), dma((2, NALL)), dma((NALL,)), dma((NALL,)),
            dma((3, NZ)), dma((3, NZ)), dma((3, NZ)), dma((3, NZ)),
            dma((2,)), dma((2,)), dma((2, NY - 1)), dma((2, NY - 1)),
            dma((2, NY)), dma((2, NY)), dma((2, NY)), dma((2, NY)),
        ],
        compiler_params=pltpu.CompilerParams(
            collective_id=0, has_side_effects=True, vmem_limit_bytes=58 * 1024 * 1024
        ),
        name="decode",
    )(
        hidden_in, norm_gains, w_qkv.reshape(COLS, 3 * INNER), w_self_out, w_cross_q, w_cross_out,
        bias, cache, memory, send_pick, recv_pick,
    )
    return hidden_out, cache_rows.transpose(0, 2, 1, 3)[:, None]


def solution(mesh):
    placed = (
        P(None, "beam", "blk"),
        P(None, "blk"),
        P("blk", None, "head"),
        P("head", "blk"),
        P("blk", "head"),
        P("head", "blk"),
        P("head", None),
        P(None, "beam", "blk", None, "head"),
        P(None, "blk", "head"),
        P(),
    )
    return jax.shard_map(
        body,
        mesh=mesh,
        in_specs=placed,
        out_specs=(P(None, "beam", "blk"), P(None, "beam", "blk", None, "head")),
        check_vma=False,
    )
```

```python
import jax
import jax.numpy as jnp
from jax import lax
from jax.experimental import pallas as pl
from jax.experimental.pallas import tpu as pltpu
from jax.sharding import PartitionSpec as P

D = 4096
EPS = 1e-06
MESH = pl.DeviceIdType.MESH
F32, BF16 = jnp.float32, jnp.bfloat16
NZ, NX, NB = 8, 2, 2
NBLK, NALL = NZ * NX, NZ * NX * NB
NY, NC = 4, 2
RB = 16
BLK = 2 * RB
ROWS = NZ * BLK
HALF = ROWS // 2
INNER = 512
COLS = 256
WIDE = 2 * COLS
SPLIT = 144
PREV = 6
CP = 2 * PREV * 2
KP = 8
LANES = 128
SLOTS = 2


def dot(a, b):
    return jnp.dot(a, b, preferred_element_type=F32)


def dot_t(a, b):
    return lax.dot_general(a, b, (((1,), (1,)), ((), ())), preferred_element_type=F32)


def iota(shape, dim):
    return lax.broadcasted_iota(jnp.int32, shape, dim)


def split3(x):
    high = x.astype(BF16).astype(F32)
    middle = (x - high).astype(BF16).astype(F32)
    return high, middle, x - high - middle


def encode(x):
    high, middle, low = split3(x)
    place = iota(x.shape, 1) & 15
    return jnp.where(place < 4, high, jnp.where(place < 8, middle, low)).astype(BF16)


def part_weight(place, lanes):
    return jnp.where(place < 8, 4.0 / lanes, 2.0 / lanes)


def decode_row():
    lane = iota((LANES, LANES), 0)
    return part_weight(lane & 15, LANES).astype(BF16)


def decode_heads():
    lane, col = iota((LANES, INNER), 0), iota((LANES, INNER), 1)
    same = ((lane >> 6) == ((col >> 6) & 1)) & (((lane >> 4) & 3) == (col >> 7))
    return jnp.where(same, part_weight(lane & 15, 16), 0.0).astype(BF16)


def piece_mask(shape, dim, pieces):
    place = (iota(shape, dim).astype(F32) + 0.5) * (1.0 / pieces)
    piece = (place - jnp.floor(place)) * pieces - 0.5
    return jnp.abs(piece - (iota(shape, 1 - dim) >> 4).astype(F32)) < 0.25


def slot_matrix(shape, dim, pieces):
    q = iota(shape, 1 - dim)
    first = ((q & (NALL - 1)) * SLOTS + (q >> 5)) * pieces
    place = iota(shape, dim)
    return jnp.where((place >= first) & (place < first + pieces), 1.0, 0.0).astype(BF16)


def spread_matrix(chosen, pieces):
    rows, cols = NALL * SLOTS * pieces, RB * pieces
    repeat = jnp.where((iota((RB, cols), 1) & 15) == iota((RB, cols), 0), 1.0, 0.0).astype(BF16)
    full = dot(slot_matrix((rows, NALL * SLOTS), 0, pieces), dot(chosen, repeat).astype(BF16))
    return jnp.where(piece_mask((rows, cols), 0, pieces), full, 0.0).astype(BF16)


def gather_matrix(chosen, pieces):
    rows, cols = RB * pieces, NALL * SLOTS * pieces
    repeat = jnp.where((iota((rows, RB), 0) & 15) == iota((rows, RB), 1), 1.0, 0.0).astype(BF16)
    full = dot(dot_t(repeat, chosen).astype(BF16), slot_matrix((NALL * SLOTS, cols), 1, pieces))
    return jnp.where(piece_mask((rows, cols), 1, pieces), full, 0.0).astype(BF16)


def picks(parents, x, z, beam):
    square = (NALL, NALL)
    o, block = iota(square, 0), iota(square, 1)
    flip_x, flip_b = (o >> 3) & 1, o >> 4
    at_offset = (beam + flip_b - 2 * beam * flip_b) * NBLK + (x + flip_x - 2 * x * flip_x) * NZ + ((z + o) & 7)
    permute = jnp.where(at_offset == block, 1.0, 0.0).astype(BF16)
    source = dot(permute, (parents >> 4).astype(F32).astype(BF16))
    local = dot(permute, (parents & 15).astype(F32).astype(BF16))
    lane = iota((NALL, RB), 1)
    slot = jnp.zeros((NALL, RB), F32)
    for k in range(RB - 1):
        slot += jnp.where((source[:, k : k + 1] == source) & (lane > k), 1.0, 0.0)
    me = (beam * NBLK + x * NZ + z).astype(F32)
    send = []
    for s in range(SLOTS):
        mine = jnp.where((source == me) & (slot == s), local, -1.0)
        send.append(sum(jnp.where(mine[:, k : k + 1] == lane.astype(F32), 1.0, 0.0) for k in range(RB)))
    own = source[:1].astype(jnp.int32)
    own_b, own_x, own_z = own >> 4, (own >> 3) & 1, own & 7
    differ_b, differ_x = jnp.abs(own_b - beam), jnp.abs(own_x - x)
    offset = differ_b * NBLK + differ_x * NZ + ((z - own_z + NZ) & 7) + slot[:1].astype(jnp.int32) * NALL
    q = iota((NALL * SLOTS, RB), 0)
    recv = jnp.where(q == offset, 1.0, 0.0)
    return jnp.concatenate(send, axis=0).astype(BF16), recv.astype(BF16)


def kernel(
    hidden, gains, wqkv, wso, wcq, wco, bias, cache, memory, parents,
    out, cache_out,
    far_hid, near_hid, far_gain, near_gain, far_wqkv, far_wso, far_wcq, far_wco, far_memory,
    hid, summed, prod, zs1, zr1, own1, zs2, zr2, own2, zs3, zr3,
    hop_send, hop_recv, kv_send, kv_recv, att, query, mixed, last_s, last_r,
    core_s, core_r, ys, yr, delta, core_s2, core_r2, ys2, yr2, delta2,
    sem_ws, sem_wr, sem_zs, sem_zr, sem_hs, sem_hr, sem_ks, sem_kr, sem_gs, sem_gr,
    sem_cs, sem_cr, sem_ys, sem_yr, sem_ds, sem_dr, sem_es, sem_er,
):
    blk, beam, head = lax.axis_index("blk"), lax.axis_index("beam"), lax.axis_index("head")
    x, z = blk // NZ, lax.rem(blk, NZ)
    y, core = head // NC, lax.rem(head, NC)

    def block_at(dx, dz):
        return (x if dx == 0 else 1 - x) * NZ + lax.rem(z + dz, NZ)

    def z_peer(dz):
        return {"blk": block_at(0, dz)}

    def all_peer(o):
        where = {"blk": block_at((o // NZ) % NX, o % NZ)}
        if o >= NBLK:
            where["beam"] = 1 - beam
        return where

    pair_peer = all_peer(NZ)
    other_peer = all_peer(NBLK + NZ)
    core_peer = {"head": y * NC + 1 - core}

    def y_peer(dy):
        return {"head": lax.rem(y + dy, NY) * NC + core}

    def remote(src, dst, send, recv, peer):
        return pltpu.make_async_remote_copy(
            src, dst, send, recv, device_id=peer, device_id_type=MESH
        )

    def rows_at(dx, dz):
        return pl.ds(pl.multiple_of(block_at(dx, dz) * RB, RB), RB)

    with jax.named_scope("entry_barrier"):
        barrier = pltpu.get_barrier_semaphore()
        peers = [all_peer(o) for o in range(1, NALL)]
        peers += [core_peer] + [y_peer(dy) for dy in range(1, NY)]
        for peer in peers:
            pl.semaphore_signal(barrier, inc=1, device_id=peer, device_id_type=MESH)
        for dz in range(NZ):
            for t in range(2):
                rows = slice(dz * BLK + t * RB, dz * BLK + (t + 1) * RB)
                far_hid[rows, :] = hidden[t, rows_at(1, dz), :]
                hid[rows, :COLS] = hidden[t, rows_at(0, dz), :]
        far_gain[...] = jnp.zeros_like(far_gain)
        far_gain[:2, :] = gains[...]
        pl.semaphore_wait(barrier, len(peers))

    pending = []

    def begin(copy):
        copy.start()
        pending.append(copy)

    my_half = pl.ds(pl.multiple_of(core * HALF, HALF), HALF)
    its_half = pl.ds(pl.multiple_of((1 - core) * HALF, HALF), HALF)

    def pair_copy(i, src, dst, peer):
        return remote(src, dst, sem_ws.at[i], sem_wr.at[i], peer)

    early = [
        pair_copy(0, far_hid.at[my_half], near_hid.at[my_half], pair_peer),
        pair_copy(1, far_gain, near_gain, pair_peer),
        pair_copy(2, wqkv.at[:, pl.ds(0, SPLIT)], far_wqkv.at[:, pl.ds(0, SPLIT)], other_peer),
        pair_copy(3, wqkv.at[:, pl.ds(SPLIT, COLS - SPLIT)], far_wqkv.at[:, pl.ds(SPLIT, COLS - SPLIT)], pair_peer),
    ]
    late = [
        pair_copy(4, wso, far_wso, other_peer),
        pair_copy(5, wcq, far_wcq, pair_peer),
        pair_copy(6, memory, far_memory, other_peer),
        pair_copy(7, wco, far_wco, pair_peer),
    ]
    for copy in early:
        begin(copy)

    def hop_copy(step, o):
        return remote(
            hop_send.at[step, o], hop_recv.at[step, o], sem_hs.at[step, o], sem_hr.at[step, o], all_peer(o)
        )

    def hop_start(step, chosen, rows):
        picked = dot(spread_matrix(chosen, CP), rows).astype(BF16)
        hop_send[step] = picked.reshape(NALL, SLOTS * CP, COLS)
        hop_recv[step, 0] = hop_send[step, 0]
        for o in range(1, NALL):
            begin(hop_copy(step, o))

    def hop_end(step, chosen):
        pick = gather_matrix(chosen, CP)
        for o in range(1, NALL):
            hop_copy(step, o).wait_recv()
        return dot(pick, hop_recv[step].reshape(NALL * SLOTS * CP, COLS)).astype(BF16)

    with jax.named_scope("cache_send"):
        send0, recv0 = picks(parents[0], x, z, beam)
        pieces = [
            cache[kv, pos, :, c * COLS : (c + 1) * COLS] for kv in range(2) for pos in range(PREV) for c in range(2)
        ]
        hop_start(0, send0, jnp.concatenate(pieces, axis=0))
        for copy in late:
            begin(copy)
        send1, recv1 = picks(parents[1], x, z, beam)

    def z_copy(phase, zs, zr, dz):
        return remote(
            zs.at[dz - 1], zr.at[dz - 1], sem_zs.at[phase, dz - 1], sem_zr.at[phase, dz - 1], z_peer(dz)
        )

    far_first = (4, 3, 5, 2, 6, 1, 7)

    def scatter_sums(phase, width, zs, zr, own):
        for dz in far_first:
            rows = slice(dz * BLK, (dz + 1) * BLK)
            zs[dz - 1, :, :width] = own[rows, :width].astype(BF16)
            zs[dz - 1, :, width:] = encode(own[rows, width:])
            begin(z_copy(phase, zs, zr, dz))
        total, squares = own[:BLK, :width], own[:BLK, width:]
        for dz in far_first[::-1]:
            z_copy(phase, zs, zr, dz).wait_recv()
            arrived = zr[dz - 1]
            total += arrived[:, :width].astype(F32)
            squares += dot(arrived[:, width:], decode_row())
        return total, lax.rsqrt(squares[:, :1] / D + EPS)

    def square_sums(states):
        return jnp.broadcast_to(jnp.sum(states * states, axis=1, keepdims=True), (ROWS, LANES))

    def gather_rows(phase, blocks):
        def copy(dz):
            back = NZ - dz
            return remote(
                blocks.at[0], blocks.at[back], sem_gs.at[phase, dz], sem_gr.at[phase, back], z_peer(dz)
            )

        for dz in far_first:
            begin(copy(dz))
        for dz in far_first[::-1]:
            remote(
                blocks.at[0], blocks.at[dz], sem_gs.at[phase, dz], sem_gr.at[phase, dz], z_peer(dz)
            ).wait_recv()
        return blocks[...].reshape(ROWS, INNER)

    quarter = HALF // NY

    def quarter_rows(half, dy):
        start = half * HALF + lax.rem(y + dy, NY) * quarter
        return pl.ds(pl.multiple_of(start, quarter), quarter)

    def head_sums(phase, core_s, core_r, ys, yr, delta):
        core_s[...] = prod[its_half, :].astype(BF16)
        copy = remote(core_s, core_r, sem_cs.at[phase], sem_cr.at[phase], core_peer)
        begin(copy)
        copy.wait_recv()
        prod[my_half, :] += core_r[...].astype(F32)

        def copy_sum(dy):
            return remote(
                ys.at[dy - 1], yr.at[dy - 1], sem_ys.at[phase, dy - 1], sem_yr.at[phase, dy - 1], y_peer(dy)
            )

        order = (2, 1, 3)
        for dy in order:
            ys[dy - 1] = prod[quarter_rows(core, dy), :].astype(BF16)
            begin(copy_sum(dy))
        total = prod[quarter_rows(core, 0), :]
        for dy in (1, 3, 2):
            copy_sum(dy).wait_recv()
            total += yr[dy - 1].astype(F32)
        delta[0, 0] = total.astype(BF16)

        def copy_y(dy):
            back = NY - dy
            return remote(
                delta.at[0, 0], delta.at[0, back], sem_ds.at[phase, dy], sem_dr.at[phase, back], y_peer(dy)
            )

        def copy_c(dy):
            return remote(
                delta.at[0, dy], delta.at[1, dy], sem_es.at[phase, dy], sem_er.at[phase, dy], core_peer
            )

        for dy in order:
            begin(copy_y(dy))
        begin(copy_c(0))
        for dy in (1, 3, 2):
            remote(
                delta.at[0, 0], delta.at[0, dy], sem_ds.at[phase, dy], sem_dr.at[phase, dy], y_peer(dy)
            ).wait_recv()
            begin(copy_c(dy))
        for dy in range(NY):
            copy_c(dy).wait_recv()
        for part in range(2):
            half = core if part == 0 else 1 - core
            for dy in range(NY):
                added = delta[part, dy].astype(F32)
                hid[quarter_rows(half, dy), :] += added
                if phase == 0:
                    summed[quarter_rows(half, dy), :] = added[:, COLS:]
                else:
                    summed[quarter_rows(half, dy), :] += added[:, COLS:]

    with jax.named_scope("qkv_products"):
        width1 = 3 * INNER
        states = hid[:, :COLS]
        normed = (states * gains[0:1, :]).astype(BF16)
        for j in range(3):
            own1[:, j * INNER : (j + 1) * INNER] = dot(normed, wqkv[j])
        own1[:, width1:] = square_sums(states)
        early[0].wait_recv()
        swap = remote(near_hid.at[my_half], near_hid.at[my_half], sem_ws.at[8], sem_wr.at[8], core_peer)
        begin(swap)
        remote(near_hid.at[my_half], near_hid.at[its_half], sem_ws.at[8], sem_wr.at[8], core_peer).wait_recv()
        early[1].wait_recv()
        states = near_hid[...]
        hid[:, COLS:] = states
        normed = (states * near_gain[0:1, :]).astype(BF16)
        own1[:, width1:] += square_sums(states)
        early[2].wait_recv()
        early[3].wait_recv()
        for j in range(3):
            own1[:, j * INNER : (j + 1) * INNER] += dot(normed, far_wqkv[j])

    with jax.named_scope("qkv_sums"):
        total, scale = scatter_sums(0, width1, zs1, zr1, own1)
        qkv = (total * scale).astype(BF16)

    with jax.named_scope("cache_forward"):
        held0 = hop_end(0, recv0)
        hop_start(1, send1, held0)

    def kv_copy(o):
        return remote(kv_send.at[o], kv_recv.at[o], sem_ks.at[o], sem_kr.at[o], all_peer(o))

    with jax.named_scope("entry_send"):
        fresh = qkv[:RB, INNER:]
        stacked = jnp.concatenate([fresh[:, p * LANES : (p + 1) * LANES] for p in range(KP)], axis=0)
        kv_send[...] = dot(spread_matrix(send1, KP), stacked).astype(BF16).reshape(NALL, SLOTS * KP, LANES)
        kv_recv[0] = kv_send[0]
        for o in range(1, NALL):
            begin(kv_copy(o))

    with jax.named_scope("cache_last"):
        held1 = hop_end(1, recv1)

    with jax.named_scope("entry_receive"):
        pick = gather_matrix(recv1, KP)
        for o in range(1, NALL):
            kv_copy(o).wait_recv()
        moved = dot(pick, kv_recv[...].reshape(NALL * SLOTS * KP, LANES)).astype(BF16)

    def side_by_side(rows, first, count):
        return jnp.concatenate([rows[(first + p) * RB : (first + p + 1) * RB] for p in range(count)], axis=1)

    with jax.named_scope("self_attention"):
        grown = []
        for t, held in enumerate((held0, held1)):
            sides = []
            for kv in range(2):
                side = [side_by_side(held, (kv * PREV + pos) * 2, 2) for pos in range(PREV)]
                if t == 1:
                    side.append(side_by_side(moved, kv * KP // 2, KP // 2))
                side.append(qkv[t * RB : (t + 1) * RB, (1 + kv) * INNER : (2 + kv) * INNER])
                sides.append(side)
            grown.append(sides)
        same_head = (iota((INNER, INNER), 0) >> 6) == (iota((INNER, INNER), 1) >> 6)
        ones = jnp.where(same_head, 1.0, 0.0).astype(BF16)
        of_head = jnp.where((iota((8, INNER), 1) >> 6) == iota((8, INNER), 0), 1.0, 0.0).astype(BF16)
        wide_bias = sum(dot(part.astype(BF16), of_head) for part in split3(bias[...]))
        for t in range(2):
            keys, values = grown[t]
            q = qkv[t * RB : (t + 1) * RB, :INNER].astype(F32) * 0.125
            products = jnp.concatenate([q * k.astype(F32) for k in keys], axis=0)
            high = products.astype(BF16)
            low = (products - high.astype(F32)).astype(BF16)
            sums = dot(high, ones) + dot(low, ones)
            last = PREV + t
            scores = [
                sums[j * RB : (j + 1) * RB] + wide_bias[last - j : last - j + 1, :] for j in range(last + 1)
            ]
            peak = scores[0]
            for s in scores[1:]:
                peak = jnp.maximum(peak, s)
            weights = [jnp.exp(s - peak) for s in scores]
            whole, acc = weights[0], weights[0].astype(BF16).astype(F32) * values[0].astype(F32)
            for w, v in zip(weights[1:], values[1:]):
                whole += w
                acc += w.astype(BF16).astype(F32) * v.astype(F32)
            att[0, t * RB : (t + 1) * RB, :] = (acc / whole).astype(BF16)

    with jax.named_scope("self_out"):
        rows = gather_rows(0, att)
        late[0].wait_recv()
        prod[:, :COLS] = dot(rows, wso[...])
        prod[:, COLS:] = dot(rows, far_wso[...])
        head_sums(0, core_s, core_r, ys, yr, delta)

    with jax.named_scope("cross_query_products"):
        states = hid[...]
        gain = jnp.concatenate([gains[1:2, :], near_gain[1:2, :]], axis=1)
        normed = (states * gain).astype(BF16)
        late[1].wait_recv()
        own2[:, :INNER] = dot(normed[:, :COLS], wcq[...]) + dot(normed[:, COLS:], far_wcq[...])
        own2[:, INNER:] = square_sums(states)

    with jax.named_scope("cross_query_sums"):
        total, scale = scatter_sums(1, INNER, zs2, zr2, own2)
        query[0] = ((total * scale).astype(BF16).astype(F32) * 0.125).astype(BF16)

    with jax.named_scope("cross_query_gather"):
        place = iota((RB * (PREV + 2), RB * (PREV + 2)), 0)
        from_row = (place & 7) * RB + (place >> 3)
        turn = jnp.where(from_row == iota(place.shape, 1), 1.0, 0.0).astype(BF16)
        queries = gather_rows(1, query)
        for kv in range(2):
            cache_out[kv] = dot(turn, jnp.concatenate(grown[1][kv], axis=0)).astype(BF16)

    with jax.named_scope("cross_partial"):
        late[2].wait_recv()
        tokens = 2 * memory.shape[1]
        low_lane = iota((tokens, LANES), 1) < 64
        low_out = iota((ROWS, LANES), 1) < 64
        one = jnp.where(low_lane, 1.0, 0.0)
        accs, lses = [], []
        for p in range(INNER // LANES):
            cols = slice(p * LANES, (p + 1) * LANES)
            k, v = (
                jnp.concatenate([memory[kv, :, cols], far_memory[kv, :, cols]], axis=0).astype(F32)
                for kv in range(2)
            )
            k2 = jnp.concatenate([jnp.where(low_lane, k, 0.0), jnp.where(low_lane, 0.0, k)], axis=0)
            v2 = jnp.concatenate(
                [
                    jnp.concatenate([jnp.where(low_lane, v, 0.0), one], axis=1),
                    jnp.concatenate([jnp.where(low_lane, 0.0, v), 1.0 - one], axis=1),
                ],
                axis=0,
            )
            scores = dot_t(queries[:, cols], k2.astype(BF16))
            peak0 = jnp.max(scores[:, :tokens], axis=1, keepdims=True)
            peak1 = jnp.max(scores[:, tokens:], axis=1, keepdims=True)
            weights = jnp.concatenate(
                [jnp.exp(scores[:, :tokens] - peak0), jnp.exp(scores[:, tokens:] - peak1)], axis=1
            )
            both = dot(weights.astype(BF16), v2.astype(BF16))
            lses.append(jnp.where(low_out, peak0, peak1) + jnp.log(both[:, LANES:]))
            acc = both[:, :LANES] / both[:, LANES:]
            accs.append(acc[:BLK])
            narrow = acc.astype(BF16)
            for dz in range(1, NZ):
                zs3[dz - 1, :, cols] = narrow[dz * BLK : (dz + 1) * BLK]
        group = (iota((ROWS, LANES), 1) >> 4) & 3
        low_pair, high_pair = jnp.where(group == 0, lses[0], lses[1]), jnp.where(group == 2, lses[2], lses[3])
        code = encode(jnp.where(group < 2, low_pair, high_pair))
        for dz in range(1, NZ):
            zs3[dz - 1, :, INNER:] = code[dz * BLK : (dz + 1) * BLK]

    with jax.named_scope("cross_join"):
        for dz in far_first:
            begin(z_copy(2, zs3, zr3, dz))
        spread_heads = decode_heads()
        peak = jnp.concatenate([lse[:BLK] for lse in lses], axis=1)
        parts = [(jnp.concatenate(accs, axis=1), peak)]
        for dz in far_first[::-1]:
            z_copy(2, zs3, zr3, dz).wait_recv()
            arrived = zr3[dz - 1]
            parts.append((arrived[:, :INNER].astype(F32), dot(arrived[:, INNER:], spread_heads)))
            peak = jnp.maximum(peak, parts[-1][1])
        weights = [jnp.exp(lse - peak) for _, lse in parts]
        acc, whole = parts[0][0] * weights[0], weights[0]
        for (a, _), w in zip(parts[1:], weights[1:]):
            acc += a * w
            whole += w
        mixed[0] = (acc / whole).astype(BF16)

    with jax.named_scope("cross_out"):
        rows = gather_rows(2, mixed)
        late[3].wait_recv()
        prod[:, :COLS] = dot(rows, wco[...])
        prod[:, COLS:] = dot(rows, far_wco[...])
        head_sums(1, core_s2, core_r2, ys2, yr2, delta2)

    with jax.named_scope("pair_columns"):
        last_s[...] = summed[...].astype(BF16)
        copy = pair_copy(9, last_s, last_r, pair_peer)
        begin(copy)
        for dz in range(NZ):
            for t in range(2):
                rows = slice(dz * BLK + t * RB, dz * BLK + (t + 1) * RB)
                out[t, rows_at(0, dz), :] = hid[rows, :COLS]
        copy.wait_recv()
        for dz in range(NZ):
            for t in range(2):
                rows = slice(dz * BLK + t * RB, dz * BLK + (t + 1) * RB)
                out[t, rows_at(1, dz), :] = far_hid[rows, :] + last_r[rows, :].astype(F32)
    for copy in pending:
        copy.wait_send()


def body(
    hidden_in, norm_gains, w_qkv, w_self_out, w_cross_q, w_cross_out, pos_bias, self_cache, memory, parents
):
    dma = pltpu.SemaphoreType.DMA
    wide1, wide2 = 3 * INNER + LANES, INNER + LANES
    half_pair = [pltpu.VMEM((HALF, WIDE), BF16)] * 2
    quarters = [pltpu.VMEM((NY - 1, HALF // NY, WIDE), BF16)] * 2
    head_buffers = [*half_pair, *quarters, pltpu.VMEM((2, NY, HALF // NY, WIDE), BF16)]
    in_vmem = pl.BlockSpec(memory_space=pltpu.VMEM)
    hidden_out, cache_rows = pl.pallas_call(
        kernel,
        out_shape=(
            jax.ShapeDtypeStruct(hidden_in.shape, F32),
            jax.ShapeDtypeStruct((2, RB * (PREV + 2), INNER), BF16),
        ),
        in_specs=[in_vmem] * 10,
        out_specs=(in_vmem, in_vmem),
        scratch_shapes=[
            pltpu.VMEM((ROWS, COLS), F32),
            pltpu.VMEM((ROWS, COLS), F32),
            pltpu.VMEM((8, COLS), F32),
            pltpu.VMEM((8, COLS), F32),
            pltpu.VMEM((3, COLS, INNER), BF16),
            pltpu.VMEM(w_self_out.shape, BF16),
            pltpu.VMEM(w_cross_q.shape, BF16),
            pltpu.VMEM(w_cross_out.shape, BF16),
            pltpu.VMEM(memory.shape, BF16),
            pltpu.VMEM((ROWS, WIDE), F32),
            pltpu.VMEM((ROWS, COLS), F32),
            pltpu.VMEM((ROWS, WIDE), F32),
            *[pltpu.VMEM((NZ - 1, BLK, wide1), BF16)] * 2,
            pltpu.VMEM((ROWS, wide1), F32),
            *[pltpu.VMEM((NZ - 1, BLK, wide2), BF16)] * 2,
            pltpu.VMEM((ROWS, wide2), F32),
            *[pltpu.VMEM((NZ - 1, BLK, wide2), BF16)] * 2,
            *[pltpu.VMEM((2, NALL, SLOTS * CP, COLS), BF16)] * 2,
            *[pltpu.VMEM((NALL, SLOTS * KP, LANES), BF16)] * 2,
            *[pltpu.VMEM((NZ, BLK, INNER), BF16)] * 3,
            *[pltpu.VMEM((ROWS, COLS), BF16)] * 2,
            *head_buffers,
            *head_buffers,
            dma((10,)), dma((10,)), dma((3, NZ - 1)), dma((3, NZ - 1)),
            dma((2, NALL)), dma((2, NALL)), dma((NALL,)), dma((NALL,)),
            dma((3, NZ)), dma((3, NZ)),
            dma((2,)), dma((2,)), dma((2, NY - 1)), dma((2, NY - 1)),
            dma((2, NY)), dma((2, NY)), dma((2, NY)), dma((2, NY)),
        ],
        compiler_params=pltpu.CompilerParams(
            collective_id=0, has_side_effects=True, vmem_limit_bytes=58 * 1024 * 1024
        ),
        name="decode",
    )(
        hidden_in, norm_gains, w_qkv.transpose(1, 0, 2), w_self_out, w_cross_q, w_cross_out, pos_bias.T,
        self_cache[:, 0].transpose(0, 2, 1, 3), memory, parents.reshape(2, NALL, RB),
    )
    return hidden_out, cache_rows.reshape(2, 1, RB, PREV + 2, INNER)


def solution(mesh):
    placed = (
        P(None, "beam", "blk"),
        P(None, "blk"),
        P("blk", None, "head"),
        P("head", "blk"),
        P("blk", "head"),
        P("head", "blk"),
        P("head", None),
        P(None, "beam", "blk", None, "head"),
        P(None, "blk", "head"),
        P(),
    )
    return jax.shard_map(
        body,
        mesh=mesh,
        in_specs=placed,
        out_specs=(P(None, "beam", "blk"), P(None, "beam", "blk", None, "head")),
        check_vma=False,
    )
```

```python
import jax
import jax.numpy as jnp
from jax import lax
from jax.experimental import pallas as pl
from jax.experimental.pallas import tpu as pltpu
from jax.sharding import PartitionSpec as P

D = 4096
EPS = 1e-06
MESH = pl.DeviceIdType.MESH
F32, BF16 = jnp.float32, jnp.bfloat16
NZ, NX, NB = 8, 2, 2
NBLK, NALL = NZ * NX, NZ * NX * NB
NY, NC = 4, 2
RB = 16
BLK = 2 * RB
ROWS = NZ * BLK
HALF = ROWS // 2
INNER = 512
COLS = 256
WIDE = 2 * COLS
SPLIT = 144
PREV = 6
CP = 2 * PREV * 2
KP = 8
LANES = 128
SLOTS = 2


def dot(a, b):
    return jnp.dot(a, b, preferred_element_type=F32)


def dot_t(a, b):
    return lax.dot_general(a, b, (((1,), (1,)), ((), ())), preferred_element_type=F32)


def iota(shape, dim):
    return lax.broadcasted_iota(jnp.int32, shape, dim)


def split3(x):
    high = x.astype(BF16).astype(F32)
    middle = (x - high).astype(BF16).astype(F32)
    return high, middle, x - high - middle


def encode(x):
    high, middle, low = split3(x)
    place = iota(x.shape, 1) & 15
    return jnp.where(place < 4, high, jnp.where(place < 8, middle, low)).astype(BF16)


def part_weight(place, lanes):
    return jnp.where(place < 8, 4.0 / lanes, 2.0 / lanes)


def decode_row():
    lane = iota((LANES, LANES), 0)
    return part_weight(lane & 15, LANES).astype(BF16)


def decode_heads():
    lane, col = iota((LANES, INNER), 0), iota((LANES, INNER), 1)
    same = ((lane >> 6) == ((col >> 6) & 1)) & (((lane >> 4) & 3) == (col >> 7))
    return jnp.where(same, part_weight(lane & 15, 16), 0.0).astype(BF16)


def piece_mask(shape, dim, pieces):
    place = (iota(shape, dim).astype(F32) + 0.5) * (1.0 / pieces)
    piece = (place - jnp.floor(place)) * pieces - 0.5
    return jnp.abs(piece - (iota(shape, 1 - dim) >> 4).astype(F32)) < 0.25


def slot_matrix(shape, dim, pieces):
    q = iota(shape, 1 - dim)
    first = ((q & (NALL - 1)) * SLOTS + (q >> 5)) * pieces
    place = iota(shape, dim)
    return jnp.where((place >= first) & (place < first + pieces), 1.0, 0.0).astype(BF16)


def spread_matrix(chosen, pieces):
    rows, cols = NALL * SLOTS * pieces, RB * pieces
    repeat = jnp.where((iota((RB, cols), 1) & 15) == iota((RB, cols), 0), 1.0, 0.0).astype(BF16)
    full = dot(slot_matrix((rows, NALL * SLOTS), 0, pieces), dot(chosen, repeat).astype(BF16))
    return jnp.where(piece_mask((rows, cols), 0, pieces), full, 0.0).astype(BF16)


def gather_matrix(chosen, pieces):
    rows, cols = RB * pieces, NALL * SLOTS * pieces
    repeat = jnp.where((iota((rows, RB), 0) & 15) == iota((rows, RB), 1), 1.0, 0.0).astype(BF16)
    full = dot(dot_t(repeat, chosen).astype(BF16), slot_matrix((NALL * SLOTS, cols), 1, pieces))
    return jnp.where(piece_mask((rows, cols), 1, pieces), full, 0.0).astype(BF16)


def piece_rows(p):
    q = iota((NALL * SLOTS, NALL * SLOTS * KP), 0)
    row = ((q & (NALL - 1)) * SLOTS + (q >> 5)) * KP + p
    return jnp.where(iota(q.shape, 1) == row, 1.0, 0.0).astype(BF16)


def head_codes(four):
    group = (iota(four[0].shape, 1) >> 4) & 3
    low_pair, high_pair = jnp.where(group == 0, four[0], four[1]), jnp.where(group == 2, four[2], four[3])
    return encode(jnp.where(group < 2, low_pair, high_pair))


def attend(q, keys, values, biases, ones):
    rows = q.shape[0]
    products = jnp.concatenate([q * k.astype(F32) for k in keys], axis=0)
    high = products.astype(BF16)
    low = (products - high.astype(F32)).astype(BF16)
    sums = dot(high, ones) + dot(low, ones)
    scores = [sums[j * rows : (j + 1) * rows] + b for j, b in enumerate(biases)]
    peak = scores[0]
    for s in scores[1:]:
        peak = jnp.maximum(peak, s)
    weights = [jnp.exp(s - peak) for s in scores]
    whole, acc = weights[0], weights[0].astype(BF16).astype(F32) * values[0].astype(F32)
    for w, v in zip(weights[1:], values[1:]):
        whole += w
        acc += w.astype(BF16).astype(F32) * v.astype(F32)
    return acc, peak, whole


def picks(parents, x, z, beam):
    square = (NALL, NALL)
    o, block = iota(square, 0), iota(square, 1)
    flip_x, flip_b = (o >> 3) & 1, o >> 4
    at_offset = (beam + flip_b - 2 * beam * flip_b) * NBLK + (x + flip_x - 2 * x * flip_x) * NZ + ((z + o) & 7)
    permute = jnp.where(at_offset == block, 1.0, 0.0).astype(BF16)
    wide = (NALL, NALL * RB)
    in_block = (iota(wide, 1) >> 4) == iota(wide, 0)
    fold = jnp.where((iota(wide[::-1][:1] + (RB,), 0) & 15) == iota(wide[::-1][:1] + (RB,), 1), 1.0, 0.0).astype(BF16)

    def folded(row):
        blocks = dot(jnp.where(in_block, row.astype(F32), 0.0).astype(BF16), fold)
        return dot(permute, blocks.astype(BF16))

    source, local = folded(parents >> 4), folded(parents & 15)
    lane = iota((NALL, RB), 1)
    slot = jnp.zeros((NALL, RB), F32)
    for k in range(RB - 1):
        slot += jnp.where((source[:, k : k + 1] == source) & (lane > k), 1.0, 0.0)
    me = (beam * NBLK + x * NZ + z).astype(F32)
    send = []
    for s in range(SLOTS):
        mine = jnp.where((source == me) & (slot == s), local, -1.0)
        send.append(sum(jnp.where(mine[:, k : k + 1] == lane.astype(F32), 1.0, 0.0) for k in range(RB)))
    own = source[:1].astype(jnp.int32)
    own_b, own_x, own_z = own >> 4, (own >> 3) & 1, own & 7
    differ_b, differ_x = jnp.abs(own_b - beam), jnp.abs(own_x - x)
    offset = differ_b * NBLK + differ_x * NZ + ((z - own_z + NZ) & 7) + slot[:1].astype(jnp.int32) * NALL
    q = iota((NALL * SLOTS, RB), 0)
    recv = jnp.where(q == offset, 1.0, 0.0)
    return jnp.concatenate(send, axis=0).astype(BF16), recv.astype(BF16)


def kernel(
    hidden, gains, wqkv_hbm, wso_hbm, wcq_hbm, wco_hbm, bias, cache, memory_hbm, parents,
    out, cache_out,
    wqkv, wso, wcq, wco, memory,
    far_hid, near_hid, far_gain, near_gain, far_wqkv, far_wso, far_wcq, far_wco, far_memory,
    hid, summed, prod, zs1, zr1, own1, zs2, zr2, own2, zs3, zr3,
    hop_send, hop_recv, kv_send, kv_recv, ask_send, ask_recv, reply_send, reply_recv, att, query, mixed, last_s, last_r,
    core_s, core_r, ys, yr, delta, core_s2, core_r2, ys2, yr2, delta2,
    sem_ws, sem_wr, sem_zs, sem_zr, sem_hs, sem_hr, sem_ks, sem_kr, sem_gs, sem_gr,
    sem_cs, sem_cr, sem_ys, sem_yr, sem_ds, sem_dr, sem_es, sem_er, sem_as, sem_ar, sem_rs, sem_rr, sem_in,
):
    blk, beam, head = lax.axis_index("blk"), lax.axis_index("beam"), lax.axis_index("head")
    x, z = blk // NZ, lax.rem(blk, NZ)
    y, core = head // NC, lax.rem(head, NC)

    def block_at(dx, dz):
        return (x if dx == 0 else 1 - x) * NZ + lax.rem(z + dz, NZ)

    def z_peer(dz):
        return {"blk": block_at(0, dz)}

    def all_peer(o):
        where = {"blk": block_at((o // NZ) % NX, o % NZ)}
        if o >= NBLK:
            where["beam"] = 1 - beam
        return where

    def back_peer(o):
        where = {"blk": block_at((o // NZ) % NX, (NZ - o) % NZ)}
        if o >= NBLK:
            where["beam"] = 1 - beam
        return where

    pair_peer = all_peer(NZ)
    other_peer = all_peer(NBLK + NZ)
    core_peer = {"head": y * NC + 1 - core}

    def y_peer(dy):
        return {"head": lax.rem(y + dy, NY) * NC + core}

    def remote(src, dst, send, recv, peer):
        return pltpu.make_async_remote_copy(
            src, dst, send, recv, device_id=peer, device_id_type=MESH
        )

    def rows_at(dx, dz):
        return pl.ds(pl.multiple_of(block_at(dx, dz) * RB, RB), RB)

    with jax.named_scope("entry_barrier"):
        barrier = pltpu.get_barrier_semaphore()
        peers = [all_peer(o) for o in range(1, NALL)]
        peers += [core_peer] + [y_peer(dy) for dy in range(1, NY)]
        for peer in peers:
            pl.semaphore_signal(barrier, inc=1, device_id=peer, device_id_type=MESH)
        inward = [
            pltpu.make_async_copy(src, dst, sem_in.at[i])
            for i, (src, dst) in enumerate(
                ((wqkv_hbm, wqkv), (wso_hbm, wso), (wcq_hbm, wcq), (memory_hbm, memory), (wco_hbm, wco))
            )
        ]
        for copy in inward:
            copy.start()
        for dz in range(NZ):
            for t in range(2):
                rows = slice(dz * BLK + t * RB, dz * BLK + (t + 1) * RB)
                far_hid[rows, :] = hidden[t, rows_at(1, dz), :]
                hid[rows, :COLS] = hidden[t, rows_at(0, dz), :]
        far_gain[...] = jnp.zeros_like(far_gain)
        far_gain[:2, :] = gains[...]

    with jax.named_scope("own_products"):
        send0, recv0 = picks(parents[0:1, :], x, z, beam)
        pieces = [
            cache[kv, pos, :, c * COLS : (c + 1) * COLS] for kv in range(2) for pos in range(PREV) for c in range(2)
        ]
        picked = dot(spread_matrix(send0, CP), jnp.concatenate(pieces, axis=0)).astype(BF16)
        hop_send[0] = picked.reshape(NALL, SLOTS * CP, COLS)
        hop_recv[0, 0] = hop_send[0, 0]
        pl.semaphore_wait(barrier, len(peers))

    pending = []

    def begin(copy):
        copy.start()
        pending.append(copy)

    my_half = pl.ds(pl.multiple_of(core * HALF, HALF), HALF)
    its_half = pl.ds(pl.multiple_of((1 - core) * HALF, HALF), HALF)

    def pair_copy(i, src, dst, peer):
        return remote(src, dst, sem_ws.at[i], sem_wr.at[i], peer)

    early = [
        pair_copy(0, far_hid.at[my_half], near_hid.at[my_half], pair_peer),
        pair_copy(1, far_gain, near_gain, pair_peer),
        pair_copy(2, wqkv_hbm.at[:, pl.ds(0, SPLIT)], far_wqkv.at[:, pl.ds(0, SPLIT)], other_peer),
        pair_copy(3, wqkv_hbm.at[:, pl.ds(SPLIT, COLS - SPLIT)], far_wqkv.at[:, pl.ds(SPLIT, COLS - SPLIT)], pair_peer),
    ]
    late = [
        pair_copy(4, wso_hbm, far_wso, other_peer),
        pair_copy(5, wcq_hbm, far_wcq, pair_peer),
        pair_copy(6, memory_hbm, far_memory, other_peer),
        pair_copy(7, wco_hbm, far_wco, pair_peer),
    ]
    for copy in early:
        begin(copy)

    def hop_copy(step, o):
        return remote(
            hop_send.at[step, o], hop_recv.at[step, o], sem_hs.at[step, o], sem_hr.at[step, o], all_peer(o)
        )

    def hop_end(step, chosen):
        pick = gather_matrix(chosen, CP)
        for o in range(1, NALL):
            hop_copy(step, o).wait_recv()
        return dot(pick, hop_recv[step].reshape(NALL * SLOTS * CP, COLS)).astype(BF16)

    with jax.named_scope("cache_send"):
        for o in range(1, NALL):
            begin(hop_copy(0, o))
        for copy in late:
            begin(copy)

    def z_copy(phase, zs, zr, dz):
        return remote(
            zs.at[dz - 1], zr.at[dz - 1], sem_zs.at[phase, dz - 1], sem_zr.at[phase, dz - 1], z_peer(dz)
        )

    far_first = (4, 3, 5, 2, 6, 1, 7)

    def scatter_sums(phase, width, zs, zr, own):
        for dz in far_first:
            rows = slice(dz * BLK, (dz + 1) * BLK)
            zs[dz - 1, :, :width] = own[rows, :width].astype(BF16)
            zs[dz - 1, :, width:] = encode(own[rows, width:])
            begin(z_copy(phase, zs, zr, dz))
        total, squares = own[:BLK, :width], own[:BLK, width:]
        for dz in far_first[::-1]:
            z_copy(phase, zs, zr, dz).wait_recv()
            arrived = zr[dz - 1]
            total += arrived[:, :width].astype(F32)
            squares += dot(arrived[:, width:], decode_row())
        return total, lax.rsqrt(squares[:, :1] / D + EPS)

    def square_sums(states):
        return jnp.broadcast_to(jnp.sum(states * states, axis=1, keepdims=True), (ROWS, LANES))

    def gather_rows(phase, blocks, meanwhile=None):
        def copy(dz):
            back = NZ - dz
            return remote(
                blocks.at[0], blocks.at[back], sem_gs.at[phase, dz], sem_gr.at[phase, back], z_peer(dz)
            )

        for dz in far_first:
            begin(copy(dz))
        if meanwhile:
            meanwhile()
        for dz in far_first[::-1]:
            remote(
                blocks.at[0], blocks.at[dz], sem_gs.at[phase, dz], sem_gr.at[phase, dz], z_peer(dz)
            ).wait_recv()
        return blocks[...].reshape(ROWS, INNER)

    quarter = HALF // NY

    def quarter_rows(half, dy):
        start = half * HALF + lax.rem(y + dy, NY) * quarter
        return pl.ds(pl.multiple_of(start, quarter), quarter)

    def head_sums(phase, core_s, core_r, ys, yr, delta, meanwhile=None):
        core_s[...] = prod[its_half, :].astype(BF16)
        copy = remote(core_s, core_r, sem_cs.at[phase], sem_cr.at[phase], core_peer)
        begin(copy)
        copy.wait_recv()
        prod[my_half, :] += core_r[...].astype(F32)

        def copy_sum(dy):
            return remote(
                ys.at[dy - 1], yr.at[dy - 1], sem_ys.at[phase, dy - 1], sem_yr.at[phase, dy - 1], y_peer(dy)
            )

        order = (2, 1, 3)
        for dy in order:
            ys[dy - 1] = prod[quarter_rows(core, dy), :].astype(BF16)
            begin(copy_sum(dy))
        if meanwhile:
            meanwhile()
        total = prod[quarter_rows(core, 0), :]
        for dy in (1, 3, 2):
            copy_sum(dy).wait_recv()
            total += yr[dy - 1].astype(F32)
        delta[0, 0] = total.astype(BF16)

        def copy_y(dy):
            back = NY - dy
            return remote(
                delta.at[0, 0], delta.at[0, back], sem_ds.at[phase, dy], sem_dr.at[phase, back], y_peer(dy)
            )

        def copy_c(dy):
            return remote(
                delta.at[0, dy], delta.at[1, dy], sem_es.at[phase, dy], sem_er.at[phase, dy], core_peer
            )

        for dy in order:
            begin(copy_y(dy))
        begin(copy_c(0))
        for dy in (1, 3, 2):
            remote(
                delta.at[0, 0], delta.at[0, dy], sem_ds.at[phase, dy], sem_dr.at[phase, dy], y_peer(dy)
            ).wait_recv()
            begin(copy_c(dy))
        for dy in range(NY):
            copy_c(dy).wait_recv()
        for part in range(2):
            half = core if part == 0 else 1 - core
            for dy in range(NY):
                added = delta[part, dy].astype(F32)
                if phase == 0:
                    hid[quarter_rows(half, dy), :] += added
                    summed[quarter_rows(half, dy), :] = added
                else:
                    summed[quarter_rows(half, dy), :] += added

    with jax.named_scope("qkv_products"):
        width1 = 3 * INNER
        states = hid[:, :COLS]
        normed = (states * gains[0:1, :]).astype(BF16)
        inward[0].wait()
        for j in range(3):
            own1[:, j * INNER : (j + 1) * INNER] = dot(normed, wqkv[j])
        own1[:, width1:] = square_sums(states)
        early[0].wait_recv()
        swap = remote(near_hid.at[my_half], near_hid.at[my_half], sem_ws.at[8], sem_wr.at[8], core_peer)
        begin(swap)
        remote(near_hid.at[my_half], near_hid.at[its_half], sem_ws.at[8], sem_wr.at[8], core_peer).wait_recv()
        early[1].wait_recv()
        states = near_hid[...]
        hid[:, COLS:] = states
        normed = (states * near_gain[0:1, :]).astype(BF16)
        own1[:, width1:] += square_sums(states)
        early[2].wait_recv()
        early[3].wait_recv()
        for j in range(3):
            own1[:, j * INNER : (j + 1) * INNER] += dot(normed, far_wqkv[j])

    with jax.named_scope("qkv_sums"):
        total, scale = scatter_sums(0, width1, zs1, zr1, own1)
        qkv = (total * scale).astype(BF16)

    def ask_copy(o):
        return remote(ask_send.at[o], ask_recv.at[o], sem_as.at[o], sem_ar.at[o], back_peer(o))

    def reply_copy(o):
        return remote(reply_send.at[o], reply_recv.at[o], sem_rs.at[o], sem_rr.at[o], all_peer(o))

    def kv_copy(o):
        return remote(kv_send.at[o], kv_recv.at[o], sem_ks.at[o], sem_kr.at[o], all_peer(o))

    def side_by_side(rows, first, count):
        return jnp.concatenate([rows[(first + p) * RB : (first + p + 1) * RB] for p in range(count)], axis=1)

    def stacked(rows):
        return [rows[:, p * LANES : (p + 1) * LANES] for p in range(rows.shape[1] // LANES)]

    def entry(t, kv):
        return qkv[t * RB : (t + 1) * RB, (1 + kv) * INNER : (2 + kv) * INNER]

    messages = (NALL, SLOTS * KP, LANES)
    flat = (NALL * SLOTS * KP, LANES)
    queries_of = [
        (qkv[t * RB : (t + 1) * RB, :INNER].astype(F32) * 0.125).astype(BF16) for t in range(2)
    ]
    with jax.named_scope("query_send"):
        send1, recv1 = picks(parents[1:2, :], x, z, beam)
        four = stacked(queries_of[1])
        asked = jnp.concatenate(four + four, axis=0)
        ask_send[...] = dot(spread_matrix(recv1, KP), asked).astype(BF16).reshape(messages)
        ask_recv[0] = ask_send[0]
        for o in range(1, NALL):
            begin(ask_copy(o))

    with jax.named_scope("parent_attention"):
        same_head = (iota((INNER, INNER), 0) >> 6) == (iota((INNER, INNER), 1) >> 6)
        ones = jnp.where(same_head, 1.0, 0.0).astype(BF16)
        of_head = jnp.where((iota((8, INNER), 1) >> 6) == iota((8, INNER), 0), 1.0, 0.0).astype(BF16)
        wide_bias = sum(
            lax.dot_general(part.astype(BF16), of_head, (((0,), (0,)), ((), ())), preferred_element_type=F32)
            for part in split3(bias[...])
        )
        held0 = hop_end(0, recv0)
        grown0 = [
            [side_by_side(held0, (kv * PREV + pos) * 2, 2) for pos in range(PREV)] + [entry(0, kv)] for kv in range(2)
        ]
        copies = [[dot(send1, rows) for rows in side] for side in grown0]
        rows_of_piece = [piece_rows(p) for p in range(5)]
        back = jnp.concatenate(rows_of_piece, axis=0)
        for o in range(1, NALL):
            ask_copy(o).wait_recv()
        arrived = ask_recv[...].reshape(flat)
        q = jnp.concatenate([dot(rows_of_piece[p], arrived) for p in range(4)], axis=1)
        last = PREV + 1
        acc, peak, whole = attend(
            q, *copies, [wide_bias[last - j : last - j + 1, :] for j in range(last)], ones
        )
        mine = (acc / whole).astype(BF16)
        lse = peak + jnp.log(whole)
        code = head_codes(stacked(lse))
        turned = lax.dot_general(
            back, jnp.concatenate(stacked(mine) + [code], axis=0), (((0,), (0,)), ((), ())), preferred_element_type=F32
        )
        reply_send[...] = turned.astype(BF16).reshape(messages)
        reply_recv[0] = reply_send[0]
        for o in range(1, NALL):
            begin(reply_copy(o))

    with jax.named_scope("self_attention"):
        acc, _, whole = attend(
            queries_of[0].astype(F32), *grown0,
            [wide_bias[PREV - j : PREV - j + 1, :] for j in range(PREV + 1)], ones,
        )
        att[0, :RB, :] = (acc / whole).astype(BF16)
        pick1 = gather_matrix(recv1, KP)
        spread_heads = decode_heads()
        fresh = queries_of[1].astype(F32) * entry(1, 0).astype(F32)
        high = fresh.astype(BF16)
        low = (fresh - high.astype(F32)).astype(BF16)
        score = dot(high, ones) + dot(low, ones) + wide_bias[0:1, :]
        for o in range(1, NALL):
            reply_copy(o).wait_recv()
        replies = dot(pick1, reply_recv[...].reshape(flat)).astype(BF16)
        lse = dot(replies[4 * RB : 5 * RB], spread_heads)
        peak = jnp.maximum(lse, score)
        w_old, w_new = jnp.exp(lse - peak), jnp.exp(score - peak)
        acc = side_by_side(replies, 0, 4).astype(F32) * w_old + w_new * entry(1, 1).astype(F32)
        att[0, RB:, :] = (acc / (w_old + w_new)).astype(BF16)

    def cache_ready():
        picked = dot(spread_matrix(send1, CP), held0).astype(BF16)
        hop_send[1] = picked.reshape(NALL, SLOTS * CP, COLS)
        hop_recv[1, 0] = hop_send[1, 0]
        added = jnp.concatenate(stacked(entry(0, 0)) + stacked(entry(0, 1)), axis=0)
        kv_send[...] = dot(spread_matrix(send1, KP), added).astype(BF16).reshape(messages)
        kv_recv[0] = kv_send[0]

    def cache_start():
        for o in range(1, NALL):
            begin(hop_copy(1, o))
            begin(kv_copy(o))

    def cache_end():
        held1 = hop_end(1, recv1)
        for o in range(1, NALL):
            kv_copy(o).wait_recv()
        moved = dot(pick1, kv_recv[...].reshape(flat)).astype(BF16)
        place = iota((RB * (PREV + 2), RB * (PREV + 2)), 0)
        from_row = (place & 7) * RB + (place >> 3)
        turn = jnp.where(from_row == iota(place.shape, 1), 1.0, 0.0).astype(BF16)
        for kv in range(2):
            side = [side_by_side(held1, (kv * PREV + pos) * 2, 2) for pos in range(PREV)]
            side += [side_by_side(moved, kv * KP // 2, KP // 2), entry(1, kv)]
            cache_out[kv] = dot(turn, jnp.concatenate(side, axis=0)).astype(BF16)

    with jax.named_scope("self_out"):
        rows = gather_rows(0, att, cache_ready)
        inward[1].wait()
        late[0].wait_recv()
        prod[:, :COLS] = dot(rows, wso[...])
        prod[:, COLS:] = dot(rows, far_wso[...])
        head_sums(0, core_s, core_r, ys, yr, delta, cache_start)

    with jax.named_scope("cross_query_products"):
        states = hid[...]
        gain = jnp.concatenate([gains[1:2, :], near_gain[1:2, :]], axis=1)
        normed = (states * gain).astype(BF16)
        inward[2].wait()
        late[1].wait_recv()
        own2[:, :INNER] = dot(normed[:, :COLS], wcq[...]) + dot(normed[:, COLS:], far_wcq[...])
        own2[:, INNER:] = square_sums(states)

    with jax.named_scope("cross_query_sums"):
        total, scale = scatter_sums(1, INNER, zs2, zr2, own2)
        query[0] = ((total * scale).astype(BF16).astype(F32) * 0.125).astype(BF16)

    with jax.named_scope("cross_query_gather"):
        queries = gather_rows(1, query)

    with jax.named_scope("cross_partial"):
        inward[3].wait()
        late[2].wait_recv()
        tokens = 2 * memory.shape[1]
        low_lane = iota((tokens, LANES), 1) < 64
        low_out = iota((ROWS, LANES), 1) < 64
        one = jnp.where(low_lane, 1.0, 0.0)
        accs, lses = [], []
        for p in range(INNER // LANES):
            cols = slice(p * LANES, (p + 1) * LANES)
            k, v = (
                jnp.concatenate([memory[kv, :, cols], far_memory[kv, :, cols]], axis=0).astype(F32)
                for kv in range(2)
            )
            k2 = jnp.concatenate([jnp.where(low_lane, k, 0.0), jnp.where(low_lane, 0.0, k)], axis=0)
            v2 = jnp.concatenate(
                [
                    jnp.concatenate([jnp.where(low_lane, v, 0.0), one], axis=1),
                    jnp.concatenate([jnp.where(low_lane, 0.0, v), 1.0 - one], axis=1),
                ],
                axis=0,
            )
            scores = dot_t(queries[:, cols], k2.astype(BF16))
            peak0 = jnp.max(scores[:, :tokens], axis=1, keepdims=True)
            peak1 = jnp.max(scores[:, tokens:], axis=1, keepdims=True)
            weights = jnp.concatenate(
                [jnp.exp(scores[:, :tokens] - peak0), jnp.exp(scores[:, tokens:] - peak1)], axis=1
            )
            both = dot(weights.astype(BF16), v2.astype(BF16))
            lses.append(jnp.where(low_out, peak0, peak1) + jnp.log(both[:, LANES:]))
            acc = both[:, :LANES] / both[:, LANES:]
            accs.append(acc[:BLK])
            narrow = acc.astype(BF16)
            for dz in range(1, NZ):
                zs3[dz - 1, :, cols] = narrow[dz * BLK : (dz + 1) * BLK]
        code = head_codes(lses)
        for dz in range(1, NZ):
            zs3[dz - 1, :, INNER:] = code[dz * BLK : (dz + 1) * BLK]

    with jax.named_scope("cross_join"):
        for dz in far_first:
            begin(z_copy(2, zs3, zr3, dz))
        peak = jnp.concatenate([lse[:BLK] for lse in lses], axis=1)
        parts = [(jnp.concatenate(accs, axis=1), peak)]
        for dz in far_first[::-1]:
            z_copy(2, zs3, zr3, dz).wait_recv()
            arrived = zr3[dz - 1]
            parts.append((arrived[:, :INNER].astype(F32), dot(arrived[:, INNER:], spread_heads)))
            peak = jnp.maximum(peak, parts[-1][1])
        weights = [jnp.exp(lse - peak) for _, lse in parts]
        acc, whole = parts[0][0] * weights[0], weights[0]
        for (a, _), w in zip(parts[1:], weights[1:]):
            acc += a * w
            whole += w
        mixed[0] = (acc / whole).astype(BF16)

    with jax.named_scope("cross_out"):
        rows = gather_rows(2, mixed, cache_end)
        inward[4].wait()
        late[3].wait_recv()
        prod[:, :COLS] = dot(rows, wco[...])
        prod[:, COLS:] = dot(rows, far_wco[...])
        head_sums(1, core_s2, core_r2, ys2, yr2, delta2)

    with jax.named_scope("pair_columns"):
        last_s[...] = summed[:, COLS:].astype(BF16)
        copy = pair_copy(9, last_s, last_r, pair_peer)
        begin(copy)
        for dz in range(NZ):
            for t in range(2):
                rows = slice(dz * BLK + t * RB, dz * BLK + (t + 1) * RB)
                out[t, rows_at(0, dz), :] = summed[rows, :COLS]
        copy.wait_recv()
        for dz in range(NZ):
            for t in range(2):
                rows = slice(dz * BLK + t * RB, dz * BLK + (t + 1) * RB)
                out[t, rows_at(1, dz), :] = last_r[rows, :].astype(F32)
    for copy in pending:
        copy.wait_send()


def body(
    hidden_in, norm_gains, w_qkv, w_self_out, w_cross_q, w_cross_out, pos_bias, self_cache, memory, parents
):
    dma = pltpu.SemaphoreType.DMA
    wide1, wide2 = 3 * INNER + LANES, INNER + LANES
    half_pair = [pltpu.VMEM((HALF, WIDE), BF16)] * 2
    quarters = [pltpu.VMEM((NY - 1, HALF // NY, WIDE), BF16)] * 2
    head_buffers = [*half_pair, *quarters, pltpu.VMEM((2, NY, HALF // NY, WIDE), BF16)]
    in_vmem = pl.BlockSpec(memory_space=pltpu.VMEM)
    in_hbm = pl.BlockSpec(memory_space=pl.ANY)
    added, cache_rows = pl.pallas_call(
        kernel,
        out_shape=(
            jax.ShapeDtypeStruct(hidden_in.shape, F32),
            jax.ShapeDtypeStruct((2, RB * (PREV + 2), INNER), BF16),
        ),
        in_specs=[in_vmem] * 2 + [in_hbm] * 4 + [in_vmem] * 2 + [in_hbm, in_vmem],
        out_specs=(in_vmem, in_vmem),
        scratch_shapes=[
            pltpu.VMEM((3, COLS, INNER), BF16),
            pltpu.VMEM(w_self_out.shape, BF16),
            pltpu.VMEM(w_cross_q.shape, BF16),
            pltpu.VMEM(w_cross_out.shape, BF16),
            pltpu.VMEM(memory.shape, BF16),
            pltpu.VMEM((ROWS, COLS), F32),
            pltpu.VMEM((ROWS, COLS), F32),
            pltpu.VMEM((8, COLS), F32),
            pltpu.VMEM((8, COLS), F32),
            pltpu.VMEM((3, COLS, INNER), BF16),
            pltpu.VMEM(w_self_out.shape, BF16),
            pltpu.VMEM(w_cross_q.shape, BF16),
            pltpu.VMEM(w_cross_out.shape, BF16),
            pltpu.VMEM(memory.shape, BF16),
            *[pltpu.VMEM((ROWS, WIDE), F32)] * 3,
            *[pltpu.VMEM((NZ - 1, BLK, wide1), BF16)] * 2,
            pltpu.VMEM((ROWS, wide1), F32),
            *[pltpu.VMEM((NZ - 1, BLK, wide2), BF16)] * 2,
            pltpu.VMEM((ROWS, wide2), F32),
            *[pltpu.VMEM((NZ - 1, BLK, wide2), BF16)] * 2,
            *[pltpu.VMEM((2, NALL, SLOTS * CP, COLS), BF16)] * 2,
            *[pltpu.VMEM((NALL, SLOTS * KP, LANES), BF16)] * 6,
            *[pltpu.VMEM((NZ, BLK, INNER), BF16)] * 3,
            *[pltpu.VMEM((ROWS, COLS), BF16)] * 2,
            *head_buffers,
            *head_buffers,
            dma((10,)), dma((10,)), dma((3, NZ - 1)), dma((3, NZ - 1)),
            dma((2, NALL)), dma((2, NALL)), dma((NALL,)), dma((NALL,)),
            dma((3, NZ)), dma((3, NZ)),
            dma((2,)), dma((2,)), dma((2, NY - 1)), dma((2, NY - 1)),
            dma((2, NY)), dma((2, NY)), dma((2, NY)), dma((2, NY)),
            dma((NALL,)), dma((NALL,)), dma((NALL,)), dma((NALL,)), dma((5,)),
        ],
        compiler_params=pltpu.CompilerParams(
            collective_id=0, has_side_effects=True, vmem_limit_bytes=58 * 1024 * 1024
        ),
        name="decode",
    )(
        hidden_in, norm_gains, w_qkv.transpose(1, 0, 2), w_self_out, w_cross_q, w_cross_out, pos_bias,
        self_cache[:, 0].transpose(0, 2, 1, 3), memory, parents,
    )
    return hidden_in + added, cache_rows.reshape(2, 1, RB, PREV + 2, INNER)


def solution(mesh):
    placed = (
        P(None, "beam", "blk"),
        P(None, "blk"),
        P("blk", None, "head"),
        P("head", "blk"),
        P("blk", "head"),
        P("head", "blk"),
        P("head", None),
        P(None, "beam", "blk", None, "head"),
        P(None, "blk", "head"),
        P(),
    )
    return jax.shard_map(
        body,
        mesh=mesh,
        in_specs=placed,
        out_specs=(P(None, "beam", "blk"), P(None, "beam", "blk", None, "head")),
        check_vma=False,
    )
```

```python
import jax
import jax.numpy as jnp
from jax import lax
from jax.experimental import pallas as pl
from jax.experimental.pallas import tpu as pltpu
from jax.sharding import PartitionSpec as P

D = 4096
EPS = 1e-06
MESH = pl.DeviceIdType.MESH
F32, BF16 = jnp.float32, jnp.bfloat16
NZ, NX, NB = 8, 2, 2
NBLK, NALL = NZ * NX, NZ * NX * NB
NY, NC = 4, 2
RB = 16
BLK = 2 * RB
ROWS = NZ * BLK
HALF = ROWS // 2
INNER = 512
COLS = 256
WIDE = 2 * COLS
SPLIT = 144
PREV = 6
CP = 2 * PREV * 2
KP = 8
GP = 16
LANES = 128
SLOTS = 2


def dot(a, b):
    return jnp.dot(a, b, preferred_element_type=F32)


def dot_t(a, b):
    return lax.dot_general(a, b, (((1,), (1,)), ((), ())), preferred_element_type=F32)


def iota(shape, dim):
    return lax.broadcasted_iota(jnp.int32, shape, dim)


def split3(x):
    high = x.astype(BF16).astype(F32)
    middle = (x - high).astype(BF16).astype(F32)
    return high, middle, x - high - middle


def encode(x):
    high, middle, low = split3(x)
    place = iota(x.shape, 1) & 15
    return jnp.where(place < 4, high, jnp.where(place < 8, middle, low)).astype(BF16)


def part_weight(place, lanes):
    return jnp.where(place < 8, 4.0 / lanes, 2.0 / lanes)


def decode_row():
    lane = iota((LANES, LANES), 0)
    return part_weight(lane & 15, LANES).astype(BF16)


def decode_heads():
    lane, col = iota((LANES, INNER), 0), iota((LANES, INNER), 1)
    same = ((lane >> 6) == ((col >> 6) & 1)) & (((lane >> 4) & 3) == (col >> 7))
    return jnp.where(same, part_weight(lane & 15, 16), 0.0).astype(BF16)


def piece_mask(shape, dim, pieces):
    place = (iota(shape, dim).astype(F32) + 0.5) * (1.0 / pieces)
    piece = (place - jnp.floor(place)) * pieces - 0.5
    return jnp.abs(piece - (iota(shape, 1 - dim) >> 4).astype(F32)) < 0.25


def slot_matrix(shape, dim, pieces):
    q = iota(shape, 1 - dim)
    first = ((q & (NALL - 1)) * SLOTS + (q >> 5)) * pieces
    place = iota(shape, dim)
    return jnp.where((place >= first) & (place < first + pieces), 1.0, 0.0).astype(BF16)


def spread_matrix(chosen, pieces):
    rows, cols = NALL * SLOTS * pieces, RB * pieces
    repeat = jnp.where((iota((RB, cols), 1) & 15) == iota((RB, cols), 0), 1.0, 0.0).astype(BF16)
    full = dot(slot_matrix((rows, NALL * SLOTS), 0, pieces), dot(chosen, repeat).astype(BF16))
    return jnp.where(piece_mask((rows, cols), 0, pieces), full, 0.0).astype(BF16)


def gather_matrix(chosen, pieces):
    rows, cols = RB * pieces, NALL * SLOTS * pieces
    repeat = jnp.where((iota((rows, RB), 0) & 15) == iota((rows, RB), 1), 1.0, 0.0).astype(BF16)
    full = dot(dot_t(repeat, chosen).astype(BF16), slot_matrix((NALL * SLOTS, cols), 1, pieces))
    return jnp.where(piece_mask((rows, cols), 1, pieces), full, 0.0).astype(BF16)


def piece_rows(p):
    q = iota((NALL * SLOTS, NALL * SLOTS * KP), 0)
    row = ((q & (NALL - 1)) * SLOTS + (q >> 5)) * KP + p
    return jnp.where(iota(q.shape, 1) == row, 1.0, 0.0).astype(BF16)


def head_codes(four):
    group = (iota(four[0].shape, 1) >> 4) & 3
    low_pair, high_pair = jnp.where(group == 0, four[0], four[1]), jnp.where(group == 2, four[2], four[3])
    return encode(jnp.where(group < 2, low_pair, high_pair))


def attend(q, keys, values, biases, ones):
    rows = q.shape[0]
    products = jnp.concatenate([q * k.astype(F32) for k in keys], axis=0)
    high = products.astype(BF16)
    low = (products - high.astype(F32)).astype(BF16)
    sums = dot(high, ones) + dot(low, ones)
    scores = [sums[j * rows : (j + 1) * rows] + b for j, b in enumerate(biases)]
    peak = scores[0]
    for s in scores[1:]:
        peak = jnp.maximum(peak, s)
    weights = [jnp.exp(s - peak) for s in scores]
    whole, acc = weights[0], weights[0].astype(BF16).astype(F32) * values[0].astype(F32)
    for w, v in zip(weights[1:], values[1:]):
        whole += w
        acc += w.astype(BF16).astype(F32) * v.astype(F32)
    return acc, peak, whole


def picks(parents, x, z, beam):
    square = (NALL, NALL)
    o, block = iota(square, 0), iota(square, 1)
    flip_x, flip_b = (o >> 3) & 1, o >> 4
    at_offset = (beam + flip_b - 2 * beam * flip_b) * NBLK + (x + flip_x - 2 * x * flip_x) * NZ + ((z + o) & 7)
    permute = jnp.where(at_offset == block, 1.0, 0.0).astype(BF16)
    wide = (NALL, NALL * RB)
    in_block = (iota(wide, 1) >> 4) == iota(wide, 0)
    fold = jnp.where((iota(wide[::-1][:1] + (RB,), 0) & 15) == iota(wide[::-1][:1] + (RB,), 1), 1.0, 0.0).astype(BF16)

    def folded(row):
        blocks = dot(jnp.where(in_block, row.astype(F32), 0.0).astype(BF16), fold)
        return dot(permute, blocks.astype(BF16))

    source, local = folded(parents >> 4), folded(parents & 15)
    lane = iota((NALL, RB), 1)
    slot = jnp.zeros((NALL, RB), F32)
    for k in range(RB - 1):
        slot += jnp.where((source[:, k : k + 1] == source) & (lane > k), 1.0, 0.0)
    me = (beam * NBLK + x * NZ + z).astype(F32)
    send = []
    for s in range(SLOTS):
        mine = jnp.where((source == me) & (slot == s), local, -1.0)
        send.append(sum(jnp.where(mine[:, k : k + 1] == lane.astype(F32), 1.0, 0.0) for k in range(RB)))
    own = source[:1].astype(jnp.int32)
    own_b, own_x, own_z = own >> 4, (own >> 3) & 1, own & 7
    differ_b, differ_x = jnp.abs(own_b - beam), jnp.abs(own_x - x)
    offset = differ_b * NBLK + differ_x * NZ + ((z - own_z + NZ) & 7) + slot[:1].astype(jnp.int32) * NALL
    q = iota((NALL * SLOTS, RB), 0)
    recv = jnp.where(q == offset, 1.0, 0.0)
    return jnp.concatenate(send, axis=0).astype(BF16), recv.astype(BF16)


def kernel(
    hidden, gains, wqkv_hbm, wso_hbm, wcq_hbm, wco_hbm, bias, cache, memory_hbm, parents,
    out, cache_out,
    wqkv, wso, wcq, wco, memory,
    far_hid, near_hid, far_gain, near_gain, far_wqkv, far_wso, far_wcq, far_wco, far_memory,
    hid, summed, prod, zs1, zr1, own1, zs2, zr2, own2, zs3, zr3,
    hop_send, hop_recv, grown_send, grown_recv, ask_send, ask_recv, reply_send, reply_recv, att, query, mixed, last_s, last_r,
    core_s, core_r, ys, yr, delta, core_s2, core_r2, ys2, yr2, delta2,
    sem_ws, sem_wr, sem_zs, sem_zr, sem_hs, sem_hr, sem_ks, sem_kr, sem_gs, sem_gr,
    sem_cs, sem_cr, sem_ys, sem_yr, sem_ds, sem_dr, sem_es, sem_er, sem_as, sem_ar, sem_rs, sem_rr, sem_in,
):
    blk, beam, head = lax.axis_index("blk"), lax.axis_index("beam"), lax.axis_index("head")
    x, z = blk // NZ, lax.rem(blk, NZ)
    y, core = head // NC, lax.rem(head, NC)

    def block_at(dx, dz):
        return (x if dx == 0 else 1 - x) * NZ + lax.rem(z + dz, NZ)

    def z_peer(dz):
        return {"blk": block_at(0, dz)}

    def all_peer(o):
        where = {"blk": block_at((o // NZ) % NX, o % NZ)}
        if o >= NBLK:
            where["beam"] = 1 - beam
        return where

    def back_peer(o):
        where = {"blk": block_at((o // NZ) % NX, (NZ - o) % NZ)}
        if o >= NBLK:
            where["beam"] = 1 - beam
        return where

    pair_peer = all_peer(NZ)
    other_peer = all_peer(NBLK + NZ)
    core_peer = {"head": y * NC + 1 - core}

    def y_peer(dy):
        return {"head": lax.rem(y + dy, NY) * NC + core}

    def remote(src, dst, send, recv, peer):
        return pltpu.make_async_remote_copy(
            src, dst, send, recv, device_id=peer, device_id_type=MESH
        )

    def rows_at(dx, dz):
        return pl.ds(pl.multiple_of(block_at(dx, dz) * RB, RB), RB)

    with jax.named_scope("entry_barrier"):
        barrier = pltpu.get_barrier_semaphore()
        peers = [all_peer(o) for o in range(1, NALL)]
        peers += [core_peer] + [y_peer(dy) for dy in range(1, NY)]
        for peer in peers:
            pl.semaphore_signal(barrier, inc=1, device_id=peer, device_id_type=MESH)
        inward = [
            pltpu.make_async_copy(src, dst, sem_in.at[i])
            for i, (src, dst) in enumerate(
                ((wqkv_hbm, wqkv), (wso_hbm, wso), (wcq_hbm, wcq), (memory_hbm, memory), (wco_hbm, wco))
            )
        ]
        for copy in inward:
            copy.start()
        for dz in range(NZ):
            for t in range(2):
                rows = slice(dz * BLK + t * RB, dz * BLK + (t + 1) * RB)
                far_hid[rows, :] = hidden[t, rows_at(1, dz), :]
                hid[rows, :COLS] = hidden[t, rows_at(0, dz), :]
        far_gain[...] = jnp.zeros_like(far_gain)
        far_gain[:2, :] = gains[...]

    with jax.named_scope("own_products"):
        send0, recv0 = picks(parents[0:1, :], x, z, beam)
        pieces = [
            cache[kv, pos, :, c * COLS : (c + 1) * COLS] for kv in range(2) for pos in range(PREV) for c in range(2)
        ]
        picked = dot(spread_matrix(send0, CP), jnp.concatenate(pieces, axis=0)).astype(BF16)
        hop_send[...] = picked.reshape(NALL, SLOTS * CP, COLS)
        hop_recv[0] = hop_send[0]
        pl.semaphore_wait(barrier, len(peers))

    pending = []

    def begin(copy):
        copy.start()
        pending.append(copy)

    my_half = pl.ds(pl.multiple_of(core * HALF, HALF), HALF)
    its_half = pl.ds(pl.multiple_of((1 - core) * HALF, HALF), HALF)

    def pair_copy(i, src, dst, peer):
        return remote(src, dst, sem_ws.at[i], sem_wr.at[i], peer)

    early = [
        pair_copy(0, far_hid.at[my_half], near_hid.at[my_half], pair_peer),
        pair_copy(1, far_gain, near_gain, pair_peer),
        pair_copy(2, wqkv_hbm.at[:, pl.ds(0, SPLIT)], far_wqkv.at[:, pl.ds(0, SPLIT)], other_peer),
        pair_copy(3, wqkv_hbm.at[:, pl.ds(SPLIT, COLS - SPLIT)], far_wqkv.at[:, pl.ds(SPLIT, COLS - SPLIT)], pair_peer),
    ]
    late = [
        pair_copy(4, wso_hbm, far_wso, other_peer),
        pair_copy(5, wcq_hbm, far_wcq, pair_peer),
        pair_copy(6, memory_hbm, far_memory, other_peer),
        pair_copy(7, wco_hbm, far_wco, pair_peer),
    ]
    for copy in early:
        begin(copy)

    def hop_copy(o):
        return remote(hop_send.at[o], hop_recv.at[o], sem_hs.at[o], sem_hr.at[o], all_peer(o))

    with jax.named_scope("cache_send"):
        for o in range(1, NALL):
            begin(hop_copy(o))

    def z_copy(phase, zs, zr, dz):
        return remote(
            zs.at[dz - 1], zr.at[dz - 1], sem_zs.at[phase, dz - 1], sem_zr.at[phase, dz - 1], z_peer(dz)
        )

    far_first = (4, 3, 5, 2, 6, 1, 7)

    def late_start():
        for copy in late:
            begin(copy)

    def scatter_sums(phase, width, zs, zr, own, meanwhile=None):
        for dz in far_first:
            rows = slice(dz * BLK, (dz + 1) * BLK)
            zs[dz - 1, :, :width] = own[rows, :width].astype(BF16)
            zs[dz - 1, :, width:] = encode(own[rows, width:])
            begin(z_copy(phase, zs, zr, dz))
        if meanwhile:
            meanwhile()
        total, squares = own[:BLK, :width], own[:BLK, width:]
        for dz in far_first[::-1]:
            z_copy(phase, zs, zr, dz).wait_recv()
            arrived = zr[dz - 1]
            total += arrived[:, :width].astype(F32)
            squares += dot(arrived[:, width:], decode_row())
        return total, lax.rsqrt(squares[:, :1] / D + EPS)

    def square_sums(states):
        return jnp.broadcast_to(jnp.sum(states * states, axis=1, keepdims=True), (ROWS, LANES))

    def gather_rows(phase, blocks, meanwhile=None):
        def copy(dz):
            back = NZ - dz
            return remote(
                blocks.at[0], blocks.at[back], sem_gs.at[phase, dz], sem_gr.at[phase, back], z_peer(dz)
            )

        for dz in far_first:
            begin(copy(dz))
        if meanwhile:
            meanwhile()
        for dz in far_first[::-1]:
            remote(
                blocks.at[0], blocks.at[dz], sem_gs.at[phase, dz], sem_gr.at[phase, dz], z_peer(dz)
            ).wait_recv()
        return blocks[...].reshape(ROWS, INNER)

    quarter = HALF // NY

    def quarter_rows(half, dy):
        start = half * HALF + lax.rem(y + dy, NY) * quarter
        return pl.ds(pl.multiple_of(start, quarter), quarter)

    def head_sums(phase, core_s, core_r, ys, yr, delta, meanwhile=None):
        core_s[...] = prod[its_half, :].astype(BF16)
        copy = remote(core_s, core_r, sem_cs.at[phase], sem_cr.at[phase], core_peer)
        begin(copy)
        copy.wait_recv()
        prod[my_half, :] += core_r[...].astype(F32)

        def copy_sum(dy):
            return remote(
                ys.at[dy - 1], yr.at[dy - 1], sem_ys.at[phase, dy - 1], sem_yr.at[phase, dy - 1], y_peer(dy)
            )

        order = (2, 1, 3)
        for dy in order:
            ys[dy - 1] = prod[quarter_rows(core, dy), :].astype(BF16)
            begin(copy_sum(dy))
        if meanwhile:
            meanwhile()
        total = prod[quarter_rows(core, 0), :]
        for dy in (1, 3, 2):
            copy_sum(dy).wait_recv()
            total += yr[dy - 1].astype(F32)
        delta[0, 0] = total.astype(BF16)

        def copy_y(dy):
            back = NY - dy
            return remote(
                delta.at[0, 0], delta.at[0, back], sem_ds.at[phase, dy], sem_dr.at[phase, back], y_peer(dy)
            )

        def copy_c(dy):
            return remote(
                delta.at[0, dy], delta.at[1, dy], sem_es.at[phase, dy], sem_er.at[phase, dy], core_peer
            )

        for dy in order:
            begin(copy_y(dy))
        begin(copy_c(0))
        for dy in (1, 3, 2):
            remote(
                delta.at[0, 0], delta.at[0, dy], sem_ds.at[phase, dy], sem_dr.at[phase, dy], y_peer(dy)
            ).wait_recv()
            begin(copy_c(dy))
        for dy in range(NY):
            copy_c(dy).wait_recv()
        for part in range(2):
            half = core if part == 0 else 1 - core
            for dy in range(NY):
                added = delta[part, dy].astype(F32)
                if phase == 0:
                    hid[quarter_rows(half, dy), :] += added
                    summed[quarter_rows(half, dy), :] = added
                else:
                    summed[quarter_rows(half, dy), :] += added

    with jax.named_scope("qkv_products"):
        width1 = 3 * INNER
        states = hid[:, :COLS]
        normed = (states * gains[0:1, :]).astype(BF16)
        inward[0].wait()
        for j in range(3):
            own1[:, j * INNER : (j + 1) * INNER] = dot(normed, wqkv[j])
        own1[:, width1:] = square_sums(states)
        early[0].wait_recv()
        swap = remote(near_hid.at[my_half], near_hid.at[my_half], sem_ws.at[8], sem_wr.at[8], core_peer)
        begin(swap)
        remote(near_hid.at[my_half], near_hid.at[its_half], sem_ws.at[8], sem_wr.at[8], core_peer).wait_recv()
        early[1].wait_recv()
        states = near_hid[...]
        hid[:, COLS:] = states
        normed = (states * near_gain[0:1, :]).astype(BF16)
        own1[:, width1:] += square_sums(states)
        early[2].wait_recv()
        early[3].wait_recv()
        for j in range(3):
            own1[:, j * INNER : (j + 1) * INNER] += dot(normed, far_wqkv[j])

    with jax.named_scope("qkv_sums"):
        total, scale = scatter_sums(0, width1, zs1, zr1, own1, late_start)
        qkv = (total * scale).astype(BF16)

    def ask_copy(o):
        return remote(ask_send.at[o], ask_recv.at[o], sem_as.at[o], sem_ar.at[o], back_peer(o))

    def reply_copy(o):
        return remote(reply_send.at[o], reply_recv.at[o], sem_rs.at[o], sem_rr.at[o], all_peer(o))

    def grown_copy(kv, o):
        return remote(
            grown_send.at[kv, o], grown_recv.at[kv, o], sem_ks.at[kv, o], sem_kr.at[kv, o], all_peer(o)
        )

    def side_by_side(rows, first, count):
        return jnp.concatenate([rows[(first + p) * RB : (first + p + 1) * RB] for p in range(count)], axis=1)

    def stacked(rows):
        return [rows[:, p * LANES : (p + 1) * LANES] for p in range(rows.shape[1] // LANES)]

    def entry(t, kv):
        return qkv[t * RB : (t + 1) * RB, (1 + kv) * INNER : (2 + kv) * INNER]

    messages = (NALL, SLOTS * KP, LANES)
    flat = (NALL * SLOTS * KP, LANES)
    queries_of = [
        (qkv[t * RB : (t + 1) * RB, :INNER].astype(F32) * 0.125).astype(BF16) for t in range(2)
    ]
    with jax.named_scope("query_send"):
        send1, recv1 = picks(parents[1:2, :], x, z, beam)
        four = stacked(queries_of[1])
        asked = jnp.concatenate(four + four, axis=0)
        ask_send[...] = dot(spread_matrix(recv1, KP), asked).astype(BF16).reshape(messages)
        ask_recv[0] = ask_send[0]
        for o in range(1, NALL):
            begin(ask_copy(o))

    with jax.named_scope("parent_attention"):
        same_head = (iota((INNER, INNER), 0) >> 6) == (iota((INNER, INNER), 1) >> 6)
        ones = jnp.where(same_head, 1.0, 0.0).astype(BF16)
        of_head = jnp.where((iota((8, INNER), 1) >> 6) == iota((8, INNER), 0), 1.0, 0.0).astype(BF16)
        wide_bias = sum(
            lax.dot_general(part.astype(BF16), of_head, (((0,), (0,)), ((), ())), preferred_element_type=F32)
            for part in split3(bias[...])
        )
        pick = gather_matrix(recv0, CP)
        for o in range(1, NALL):
            hop_copy(o).wait_recv()
        held0 = dot(pick, hop_recv[...].reshape(NALL * SLOTS * CP, COLS)).astype(BF16)
        grown0 = [
            [side_by_side(held0, (kv * PREV + pos) * 2, 2) for pos in range(PREV)] + [entry(0, kv)] for kv in range(2)
        ]
        copies = [[dot(send1, rows) for rows in side] for side in grown0]
        rows_of_piece = [piece_rows(p) for p in range(5)]
        back = jnp.concatenate(rows_of_piece, axis=0)
        for o in range(1, NALL):
            ask_copy(o).wait_recv()
        arrived = ask_recv[...].reshape(flat)
        q = jnp.concatenate([dot(rows_of_piece[p], arrived) for p in range(4)], axis=1)
        last = PREV + 1
        acc, peak, whole = attend(
            q, *copies, [wide_bias[last - j : last - j + 1, :] for j in range(last)], ones
        )
        mine = (acc / whole).astype(BF16)
        lse = peak + jnp.log(whole)
        code = head_codes(stacked(lse))
        turned = lax.dot_general(
            back, jnp.concatenate(stacked(mine) + [code], axis=0), (((0,), (0,)), ((), ())), preferred_element_type=F32
        )
        reply_send[...] = turned.astype(BF16).reshape(messages)
        reply_recv[0] = reply_send[0]
        for o in range(1, NALL):
            begin(reply_copy(o))

    with jax.named_scope("self_attention"):
        acc, _, whole = attend(
            queries_of[0].astype(F32), *grown0,
            [wide_bias[PREV - j : PREV - j + 1, :] for j in range(PREV + 1)], ones,
        )
        att[0, :RB, :] = (acc / whole).astype(BF16)
        pick1 = gather_matrix(recv1, KP)
        spread_heads = decode_heads()
        fresh = queries_of[1].astype(F32) * entry(1, 0).astype(F32)
        high = fresh.astype(BF16)
        low = (fresh - high.astype(F32)).astype(BF16)
        score = dot(high, ones) + dot(low, ones) + wide_bias[0:1, :]
        for o in range(1, NALL):
            reply_copy(o).wait_recv()
        replies = dot(pick1, reply_recv[...].reshape(flat)).astype(BF16)
        lse = dot(replies[4 * RB : 5 * RB], spread_heads)
        peak = jnp.maximum(lse, score)
        w_old, w_new = jnp.exp(lse - peak), jnp.exp(score - peak)
        acc = side_by_side(replies, 0, 4).astype(F32) * w_old + w_new * entry(1, 1).astype(F32)
        att[0, RB:, :] = (acc / (w_old + w_new)).astype(BF16)

    def cache_ready():
        spread = spread_matrix(send1, GP)
        for kv in range(2):
            new = entry(0, kv)
            halves = [new[:, :COLS], new[:, COLS:]]
            first = kv * PREV * 2 * RB
            rows = jnp.concatenate([held0[first : first + PREV * 2 * RB], *halves, *halves], axis=0)
            grown_send[kv] = dot(spread, rows).astype(BF16).reshape(NALL, SLOTS * GP, COLS)
            grown_recv[kv, 0] = grown_send[kv, 0]

    def cache_start(kv):
        for o in range(1, NALL):
            begin(grown_copy(kv, o))

    def cache_end():
        pick = gather_matrix(recv1, GP)
        place = iota((RB * (PREV + 2), RB * (PREV + 2)), 0)
        from_row = (place & 7) * RB + (place >> 3)
        turn = jnp.where(from_row == iota(place.shape, 1), 1.0, 0.0).astype(BF16)
        for kv in range(2):
            for o in range(1, NALL):
                grown_copy(kv, o).wait_recv()
            held1 = dot(pick, grown_recv[kv].reshape(NALL * SLOTS * GP, COLS)).astype(BF16)
            side = [side_by_side(held1, pos * 2, 2) for pos in range(PREV + 1)] + [entry(1, kv)]
            cache_out[kv] = dot(turn, jnp.concatenate(side, axis=0)).astype(BF16)

    with jax.named_scope("self_out"):
        rows = gather_rows(0, att, cache_ready)
        inward[1].wait()
        late[0].wait_recv()
        prod[:, :COLS] = dot(rows, wso[...])
        prod[:, COLS:] = dot(rows, far_wso[...])
        head_sums(0, core_s, core_r, ys, yr, delta, lambda: cache_start(0))

    with jax.named_scope("cross_query_products"):
        states = hid[...]
        gain = jnp.concatenate([gains[1:2, :], near_gain[1:2, :]], axis=1)
        normed = (states * gain).astype(BF16)
        inward[2].wait()
        late[1].wait_recv()
        own2[:, :INNER] = dot(normed[:, :COLS], wcq[...]) + dot(normed[:, COLS:], far_wcq[...])
        own2[:, INNER:] = square_sums(states)

    with jax.named_scope("cross_query_sums"):
        total, scale = scatter_sums(1, INNER, zs2, zr2, own2)
        query[0] = ((total * scale).astype(BF16).astype(F32) * 0.125).astype(BF16)

    with jax.named_scope("cross_query_gather"):
        queries = gather_rows(1, query)

    with jax.named_scope("cross_partial"):
        inward[3].wait()
        late[2].wait_recv()
        tokens = 2 * memory.shape[1]
        low_lane = iota((tokens, LANES), 1) < 64
        low_out = iota((ROWS, LANES), 1) < 64
        one = jnp.where(low_lane, 1.0, 0.0)
        accs, lses = [], []
        for p in range(INNER // LANES):
            cols = slice(p * LANES, (p + 1) * LANES)
            k, v = (
                jnp.concatenate([memory[kv, :, cols], far_memory[kv, :, cols]], axis=0).astype(F32)
                for kv in range(2)
            )
            k2 = jnp.concatenate([jnp.where(low_lane, k, 0.0), jnp.where(low_lane, 0.0, k)], axis=0)
            v2 = jnp.concatenate(
                [
                    jnp.concatenate([jnp.where(low_lane, v, 0.0), one], axis=1),
                    jnp.concatenate([jnp.where(low_lane, 0.0, v), 1.0 - one], axis=1),
                ],
                axis=0,
            )
            scores = dot_t(queries[:, cols], k2.astype(BF16))
            peak0 = jnp.max(scores[:, :tokens], axis=1, keepdims=True)
            peak1 = jnp.max(scores[:, tokens:], axis=1, keepdims=True)
            weights = jnp.concatenate(
                [jnp.exp(scores[:, :tokens] - peak0), jnp.exp(scores[:, tokens:] - peak1)], axis=1
            )
            both = dot(weights.astype(BF16), v2.astype(BF16))
            lses.append(jnp.where(low_out, peak0, peak1) + jnp.log(both[:, LANES:]))
            acc = both[:, :LANES] / both[:, LANES:]
            accs.append(acc[:BLK])
            narrow = acc.astype(BF16)
            for dz in range(1, NZ):
                zs3[dz - 1, :, cols] = narrow[dz * BLK : (dz + 1) * BLK]
        code = head_codes(lses)
        for dz in range(1, NZ):
            zs3[dz - 1, :, INNER:] = code[dz * BLK : (dz + 1) * BLK]

    with jax.named_scope("cross_join"):
        for dz in far_first:
            begin(z_copy(2, zs3, zr3, dz))
        peak = jnp.concatenate([lse[:BLK] for lse in lses], axis=1)
        parts = [(jnp.concatenate(accs, axis=1), peak)]
        for dz in far_first[::-1]:
            z_copy(2, zs3, zr3, dz).wait_recv()
            arrived = zr3[dz - 1]
            parts.append((arrived[:, :INNER].astype(F32), dot(arrived[:, INNER:], spread_heads)))
            peak = jnp.maximum(peak, parts[-1][1])
        weights = [jnp.exp(lse - peak) for _, lse in parts]
        acc, whole = parts[0][0] * weights[0], weights[0]
        for (a, _), w in zip(parts[1:], weights[1:]):
            acc += a * w
            whole += w
        mixed[0] = (acc / whole).astype(BF16)

    with jax.named_scope("cross_out"):
        rows = gather_rows(2, mixed)
        inward[4].wait()
        late[3].wait_recv()
        prod[:, :COLS] = dot(rows, wco[...])
        prod[:, COLS:] = dot(rows, far_wco[...])
        head_sums(1, core_s2, core_r2, ys2, yr2, delta2, lambda: cache_start(1))

    with jax.named_scope("pair_columns"):
        last_s[...] = summed[:, COLS:].astype(BF16)
        copy = pair_copy(9, last_s, last_r, pair_peer)
        begin(copy)
        cache_end()
        for dz in range(NZ):
            for t in range(2):
                rows = slice(dz * BLK + t * RB, dz * BLK + (t + 1) * RB)
                out[t, rows_at(0, dz), :] = summed[rows, :COLS]
        copy.wait_recv()
        for dz in range(NZ):
            for t in range(2):
                rows = slice(dz * BLK + t * RB, dz * BLK + (t + 1) * RB)
                out[t, rows_at(1, dz), :] = last_r[rows, :].astype(F32)
    for copy in pending:
        copy.wait_send()


def body(
    hidden_in, norm_gains, w_qkv, w_self_out, w_cross_q, w_cross_out, pos_bias, self_cache, memory, parents
):
    dma = pltpu.SemaphoreType.DMA
    wide1, wide2 = 3 * INNER + LANES, INNER + LANES
    half_pair = [pltpu.VMEM((HALF, WIDE), BF16)] * 2
    quarters = [pltpu.VMEM((NY - 1, HALF // NY, WIDE), BF16)] * 2
    head_buffers = [*half_pair, *quarters, pltpu.VMEM((2, NY, HALF // NY, WIDE), BF16)]
    in_vmem = pl.BlockSpec(memory_space=pltpu.VMEM)
    in_hbm = pl.BlockSpec(memory_space=pl.ANY)
    added, cache_rows = pl.pallas_call(
        kernel,
        out_shape=(
            jax.ShapeDtypeStruct(hidden_in.shape, F32),
            jax.ShapeDtypeStruct((2, RB * (PREV + 2), INNER), BF16),
        ),
        in_specs=[in_vmem] * 2 + [in_hbm] * 4 + [in_vmem] * 2 + [in_hbm, in_vmem],
        out_specs=(in_vmem, in_vmem),
        scratch_shapes=[
            pltpu.VMEM((3, COLS, INNER), BF16),
            pltpu.VMEM(w_self_out.shape, BF16),
            pltpu.VMEM(w_cross_q.shape, BF16),
            pltpu.VMEM(w_cross_out.shape, BF16),
            pltpu.VMEM(memory.shape, BF16),
            pltpu.VMEM((ROWS, COLS), F32),
            pltpu.VMEM((ROWS, COLS), F32),
            pltpu.VMEM((8, COLS), F32),
            pltpu.VMEM((8, COLS), F32),
            pltpu.VMEM((3, COLS, INNER), BF16),
            pltpu.VMEM(w_self_out.shape, BF16),
            pltpu.VMEM(w_cross_q.shape, BF16),
            pltpu.VMEM(w_cross_out.shape, BF16),
            pltpu.VMEM(memory.shape, BF16),
            *[pltpu.VMEM((ROWS, WIDE), F32)] * 3,
            *[pltpu.VMEM((NZ - 1, BLK, wide1), BF16)] * 2,
            pltpu.VMEM((ROWS, wide1), F32),
            *[pltpu.VMEM((NZ - 1, BLK, wide2), BF16)] * 2,
            pltpu.VMEM((ROWS, wide2), F32),
            *[pltpu.VMEM((NZ - 1, BLK, wide2), BF16)] * 2,
            *[pltpu.VMEM((NALL, SLOTS * CP, COLS), BF16)] * 2,
            *[pltpu.VMEM((2, NALL, SLOTS * GP, COLS), BF16)] * 2,
            *[pltpu.VMEM((NALL, SLOTS * KP, LANES), BF16)] * 4,
            *[pltpu.VMEM((NZ, BLK, INNER), BF16)] * 3,
            *[pltpu.VMEM((ROWS, COLS), BF16)] * 2,
            *head_buffers,
            *head_buffers,
            dma((10,)), dma((10,)), dma((3, NZ - 1)), dma((3, NZ - 1)),
            dma((NALL,)), dma((NALL,)), dma((2, NALL)), dma((2, NALL)),
            dma((3, NZ)), dma((3, NZ)),
            dma((2,)), dma((2,)), dma((2, NY - 1)), dma((2, NY - 1)),
            dma((2, NY)), dma((2, NY)), dma((2, NY)), dma((2, NY)),
            dma((NALL,)), dma((NALL,)), dma((NALL,)), dma((NALL,)), dma((5,)),
        ],
        compiler_params=pltpu.CompilerParams(
            collective_id=0, has_side_effects=True, vmem_limit_bytes=58 * 1024 * 1024
        ),
        name="decode",
    )(
        hidden_in, norm_gains, w_qkv.transpose(1, 0, 2), w_self_out, w_cross_q, w_cross_out, pos_bias,
        self_cache[:, 0].transpose(0, 2, 1, 3), memory, parents,
    )
    return hidden_in + added, cache_rows.reshape(2, 1, RB, PREV + 2, INNER)


def solution(mesh):
    placed = (
        P(None, "beam", "blk"),
        P(None, "blk"),
        P("blk", None, "head"),
        P("head", "blk"),
        P("blk", "head"),
        P("head", "blk"),
        P("head", None),
        P(None, "beam", "blk", None, "head"),
        P(None, "blk", "head"),
        P(),
    )
    return jax.shard_map(
        body,
        mesh=mesh,
        in_specs=placed,
        out_specs=(P(None, "beam", "blk"), P(None, "beam", "blk", None, "head")),
        check_vma=False,
    )
```

```python
import jax
import jax.numpy as jnp
from jax import lax
from jax.experimental import pallas as pl
from jax.experimental.pallas import tpu as pltpu
from jax.sharding import PartitionSpec as P

D = 4096
EPS = 1e-06
MESH = pl.DeviceIdType.MESH
F32, BF16 = jnp.float32, jnp.bfloat16
NZ, NX, NB = 8, 2, 2
NBLK, NALL = NZ * NX, NZ * NX * NB
NY, NC = 4, 2
RB = 16
BLK = 2 * RB
ROWS = NZ * BLK
HALF = ROWS // 2
STREAM = ROWS // 2
INNER = 512
COLS = 256
WIDE = 2 * COLS
SPLIT = 144
PREV = 6
CP = 2 * PREV * 2
KP = 8
GP = 16
LANES = 128
SLOTS = 2


def dot(a, b):
    return jnp.dot(a, b, preferred_element_type=F32)


def dot_t(a, b):
    return lax.dot_general(a, b, (((1,), (1,)), ((), ())), preferred_element_type=F32)


def iota(shape, dim):
    return lax.broadcasted_iota(jnp.int32, shape, dim)


def split3(x):
    high = x.astype(BF16).astype(F32)
    middle = (x - high).astype(BF16).astype(F32)
    return high, middle, x - high - middle


def encode(x):
    high, middle, low = split3(x)
    place = iota(x.shape, 1) & 15
    return jnp.where(place < 4, high, jnp.where(place < 8, middle, low)).astype(BF16)


def part_weight(place, lanes):
    return jnp.where(place < 8, 4.0 / lanes, 2.0 / lanes)


def decode_row():
    lane = iota((LANES, LANES), 0)
    return part_weight(lane & 15, LANES).astype(BF16)


def decode_heads():
    lane, col = iota((LANES, INNER), 0), iota((LANES, INNER), 1)
    same = ((lane >> 6) == ((col >> 6) & 1)) & (((lane >> 4) & 3) == (col >> 7))
    return jnp.where(same, part_weight(lane & 15, 16), 0.0).astype(BF16)


def piece_mask(shape, dim, pieces):
    place = (iota(shape, dim).astype(F32) + 0.5) * (1.0 / pieces)
    piece = (place - jnp.floor(place)) * pieces - 0.5
    return jnp.abs(piece - (iota(shape, 1 - dim) >> 4).astype(F32)) < 0.25


def slot_matrix(shape, dim, pieces):
    q = iota(shape, 1 - dim)
    first = ((q & (NALL - 1)) * SLOTS + (q >> 5)) * pieces
    place = iota(shape, dim)
    return jnp.where((place >= first) & (place < first + pieces), 1.0, 0.0).astype(BF16)


def spread_matrix(chosen, pieces):
    rows, cols = NALL * SLOTS * pieces, RB * pieces
    repeat = jnp.where((iota((RB, cols), 1) & 15) == iota((RB, cols), 0), 1.0, 0.0).astype(BF16)
    full = dot(slot_matrix((rows, NALL * SLOTS), 0, pieces), dot(chosen, repeat).astype(BF16))
    return jnp.where(piece_mask((rows, cols), 0, pieces), full, 0.0).astype(BF16)


def gather_matrix(chosen, pieces):
    rows, cols = RB * pieces, NALL * SLOTS * pieces
    repeat = jnp.where((iota((rows, RB), 0) & 15) == iota((rows, RB), 1), 1.0, 0.0).astype(BF16)
    full = dot(dot_t(repeat, chosen).astype(BF16), slot_matrix((NALL * SLOTS, cols), 1, pieces))
    return jnp.where(piece_mask((rows, cols), 1, pieces), full, 0.0).astype(BF16)


def piece_rows(p):
    q = iota((NALL * SLOTS, NALL * SLOTS * KP), 0)
    row = ((q & (NALL - 1)) * SLOTS + (q >> 5)) * KP + p
    return jnp.where(iota(q.shape, 1) == row, 1.0, 0.0).astype(BF16)


def head_codes(four):
    group = (iota(four[0].shape, 1) >> 4) & 3
    low_pair, high_pair = jnp.where(group == 0, four[0], four[1]), jnp.where(group == 2, four[2], four[3])
    return encode(jnp.where(group < 2, low_pair, high_pair))


def attend(q, keys, values, biases, ones):
    rows = q.shape[0]
    products = jnp.concatenate([q * k.astype(F32) for k in keys], axis=0)
    high = products.astype(BF16)
    low = (products - high.astype(F32)).astype(BF16)
    sums = dot(high, ones) + dot(low, ones)
    scores = [sums[j * rows : (j + 1) * rows] + b for j, b in enumerate(biases)]
    peak = scores[0]
    for s in scores[1:]:
        peak = jnp.maximum(peak, s)
    weights = [jnp.exp(s - peak) for s in scores]
    whole, acc = weights[0], weights[0].astype(BF16).astype(F32) * values[0].astype(F32)
    for w, v in zip(weights[1:], values[1:]):
        whole += w
        acc += w.astype(BF16).astype(F32) * v.astype(F32)
    return acc, peak, whole


def picks(parents, x, z, beam):
    square = (NALL, NALL)
    o, block = iota(square, 0), iota(square, 1)
    flip_x, flip_b = (o >> 3) & 1, o >> 4
    at_offset = (beam + flip_b - 2 * beam * flip_b) * NBLK + (x + flip_x - 2 * x * flip_x) * NZ + ((z + o) & 7)
    permute = jnp.where(at_offset == block, 1.0, 0.0).astype(BF16)
    wide = (NALL, NALL * RB)
    in_block = (iota(wide, 1) >> 4) == iota(wide, 0)
    fold = jnp.where((iota(wide[::-1][:1] + (RB,), 0) & 15) == iota(wide[::-1][:1] + (RB,), 1), 1.0, 0.0).astype(BF16)

    def folded(row):
        blocks = dot(jnp.where(in_block, row.astype(F32), 0.0).astype(BF16), fold)
        return dot(permute, blocks.astype(BF16))

    source, local = folded(parents >> 4), folded(parents & 15)
    lane = iota((NALL, RB), 1)
    slot = jnp.zeros((NALL, RB), F32)
    for k in range(RB - 1):
        slot += jnp.where((source[:, k : k + 1] == source) & (lane > k), 1.0, 0.0)
    me = (beam * NBLK + x * NZ + z).astype(F32)
    send = []
    for s in range(SLOTS):
        mine = jnp.where((source == me) & (slot == s), local, -1.0)
        send.append(sum(jnp.where(mine[:, k : k + 1] == lane.astype(F32), 1.0, 0.0) for k in range(RB)))
    own = source[:1].astype(jnp.int32)
    own_b, own_x, own_z = own >> 4, (own >> 3) & 1, own & 7
    differ_b, differ_x = jnp.abs(own_b - beam), jnp.abs(own_x - x)
    offset = differ_b * NBLK + differ_x * NZ + ((z - own_z + NZ) & 7) + slot[:1].astype(jnp.int32) * NALL
    q = iota((NALL * SLOTS, RB), 0)
    recv = jnp.where(q == offset, 1.0, 0.0)
    return jnp.concatenate(send, axis=0).astype(BF16), recv.astype(BF16)


def kernel(
    hidden, gains, wqkv_hbm, wso_hbm, wcq_hbm, wco_hbm, bias, cache, memory_hbm, parents,
    out, cache_out,
    wqkv, wso, wcq, wco, memory,
    far_hid, near_hid, far_gain, near_gain, far_wqkv, far_wso, far_wcq, far_wco, far_memory,
    hid, summed, prod, zs1, zr1, own1, zs2, zr2, own2, zs3, zr3,
    hop_send, hop_recv, grown_send, grown_recv, ask_send, ask_recv, reply_send, reply_recv, att, query, mixed, last_s, last_r,
    core_s, core_r, ys, yr, delta, core_s2, core_r2, ys2, yr2, delta2,
    sem_ws, sem_wr, sem_zs, sem_zr, sem_hs, sem_hr, sem_ks, sem_kr, sem_gs, sem_gr,
    sem_cs, sem_cr, sem_ys, sem_yr, sem_ds, sem_dr, sem_es, sem_er, sem_as, sem_ar, sem_rs, sem_rr, sem_in,
):
    blk, beam, head = lax.axis_index("blk"), lax.axis_index("beam"), lax.axis_index("head")
    x, z = blk // NZ, lax.rem(blk, NZ)
    y, core = head // NC, lax.rem(head, NC)

    def block_at(dx, dz):
        return (x if dx == 0 else 1 - x) * NZ + lax.rem(z + dz, NZ)

    def z_peer(dz):
        return {"blk": block_at(0, dz)}

    def all_peer(o):
        where = {"blk": block_at((o // NZ) % NX, o % NZ)}
        if o >= NBLK:
            where["beam"] = 1 - beam
        return where

    def back_peer(o):
        where = {"blk": block_at((o // NZ) % NX, (NZ - o) % NZ)}
        if o >= NBLK:
            where["beam"] = 1 - beam
        return where

    pair_peer = all_peer(NZ)
    other_peer = all_peer(NBLK + NZ)
    core_peer = {"head": y * NC + 1 - core}

    def y_peer(dy):
        return {"head": lax.rem(y + dy, NY) * NC + core}

    def remote(src, dst, send, recv, peer):
        return pltpu.make_async_remote_copy(
            src, dst, send, recv, device_id=peer, device_id_type=MESH
        )

    def rows_at(dx, dz):
        return pl.ds(pl.multiple_of(block_at(dx, dz) * RB, RB), RB)

    with jax.named_scope("entry_barrier"):
        barrier = pltpu.get_barrier_semaphore()
        peers = [all_peer(o) for o in range(1, NALL)]
        peers += [core_peer] + [y_peer(dy) for dy in range(1, NY)]
        for peer in peers:
            pl.semaphore_signal(barrier, inc=1, device_id=peer, device_id_type=MESH)
        inward = [
            pltpu.make_async_copy(src, dst, sem_in.at[i])
            for i, (src, dst) in enumerate(
                ((wqkv_hbm, wqkv), (wso_hbm, wso), (wcq_hbm, wcq), (memory_hbm, memory), (wco_hbm, wco))
            )
        ]
        for copy in inward:
            copy.start()
        for dz in range(NZ):
            for t in range(2):
                rows = slice(dz * BLK + t * RB, dz * BLK + (t + 1) * RB)
                far_hid[rows, :] = hidden[t, rows_at(1, dz), :]
                hid[rows, :COLS] = hidden[t, rows_at(0, dz), :]
        far_gain[...] = jnp.zeros_like(far_gain)
        far_gain[:2, :] = gains[...]

    with jax.named_scope("own_products"):
        send0, recv0 = picks(parents[0:1, :], x, z, beam)
        pieces = [
            cache[kv, pos, :, c * COLS : (c + 1) * COLS] for kv in range(2) for pos in range(PREV) for c in range(2)
        ]
        picked = dot(spread_matrix(send0, CP), jnp.concatenate(pieces, axis=0)).astype(BF16)
        hop_send[...] = picked.reshape(NALL, SLOTS * CP, COLS)
        hop_recv[0] = hop_send[0]
        pl.semaphore_wait(barrier, len(peers))

    pending = []

    def begin(copy):
        copy.start()
        pending.append(copy)

    my_half = pl.ds(pl.multiple_of(core * HALF, HALF), HALF)
    its_half = pl.ds(pl.multiple_of((1 - core) * HALF, HALF), HALF)

    def pair_copy(i, src, dst, peer):
        return remote(src, dst, sem_ws.at[i], sem_wr.at[i], peer)

    early = [
        pair_copy(0, far_hid.at[my_half], near_hid.at[my_half], pair_peer),
        pair_copy(1, far_gain, near_gain, pair_peer),
        pair_copy(2, wqkv_hbm.at[:, pl.ds(0, SPLIT)], far_wqkv.at[:, pl.ds(0, SPLIT)], other_peer),
        pair_copy(3, wqkv_hbm.at[:, pl.ds(SPLIT, COLS - SPLIT)], far_wqkv.at[:, pl.ds(SPLIT, COLS - SPLIT)], pair_peer),
    ]
    late = [
        pair_copy(4, wso_hbm, far_wso, other_peer),
        pair_copy(5, wcq_hbm, far_wcq, pair_peer),
        pair_copy(6, memory_hbm, far_memory, other_peer),
        pair_copy(7, wco_hbm, far_wco, pair_peer),
    ]
    for copy in early:
        begin(copy)

    def hop_copy(o):
        return remote(hop_send.at[o], hop_recv.at[o], sem_hs.at[o], sem_hr.at[o], all_peer(o))

    with jax.named_scope("cache_send"):
        for o in range(1, NALL):
            begin(hop_copy(o))

    def z_copy(phase, zs, zr, dz):
        return remote(
            zs.at[dz - 1], zr.at[dz - 1], sem_zs.at[phase, dz - 1], sem_zr.at[phase, dz - 1], z_peer(dz)
        )

    far_first = (4, 3, 5, 2, 6, 1, 7)

    def late_start():
        for copy in late:
            begin(copy)

    def scatter_start(i, width, size, zs, zr, own):
        for dz in far_first:
            rows = slice(dz * size, (dz + 1) * size)
            zs[dz - 1, :, :width] = own[rows, :width].astype(BF16)
            zs[dz - 1, :, width:] = encode(own[rows, width:])
            begin(z_copy(i, zs, zr, dz))

    def scatter_end(i, width, size, zs, zr, own):
        total, squares = own[:size, :width], own[:size, width:]
        for dz in far_first[::-1]:
            z_copy(i, zs, zr, dz).wait_recv()
            arrived = zr[dz - 1]
            total += arrived[:, :width].astype(F32)
            squares += dot(arrived[:, width:], decode_row())
        return total, lax.rsqrt(squares[:, :1] / D + EPS)

    def square_sums(states):
        return jnp.broadcast_to(jnp.sum(states * states, axis=1, keepdims=True), (states.shape[0], LANES))

    def gather_start(i, blocks):
        for dz in far_first:
            back = NZ - dz
            begin(remote(blocks.at[0], blocks.at[back], sem_gs.at[i, dz], sem_gr.at[i, back], z_peer(dz)))

    def gather_end(i, blocks):
        for dz in far_first[::-1]:
            remote(blocks.at[0], blocks.at[dz], sem_gs.at[i, dz], sem_gr.at[i, dz], z_peer(dz)).wait_recv()
        return blocks[...].reshape(STREAM, INNER)

    part_rows = STREAM // 2
    quarter = part_rows // NY
    order, nearest = (2, 1, 3), (1, 3, 2)

    def quarter_rows(half, dy):
        start = half * part_rows + lax.rem(y + dy, NY) * quarter
        return pl.ds(pl.multiple_of(start, quarter), quarter)

    def half_rows(half):
        return pl.ds(pl.multiple_of(half * part_rows, part_rows), part_rows)

    def head_sums(i, first, product, total_out, core_s, core_r, ys, yr, delta, meanwhile):
        core_s[...] = product[half_rows(1 - core), :].astype(BF16)
        copy = remote(core_s, core_r, sem_cs.at[i], sem_cr.at[i], core_peer)
        begin(copy)
        yield
        copy.wait_recv()
        product[half_rows(core), :] += core_r[...].astype(F32)

        def copy_sum(dy):
            return remote(
                ys.at[dy - 1], yr.at[dy - 1], sem_ys.at[i, dy - 1], sem_yr.at[i, dy - 1], y_peer(dy)
            )

        for dy in order:
            ys[dy - 1] = product[quarter_rows(core, dy), :].astype(BF16)
            begin(copy_sum(dy))
        meanwhile()
        yield
        total = product[quarter_rows(core, 0), :]
        for dy in nearest:
            copy_sum(dy).wait_recv()
            total += yr[dy - 1].astype(F32)
        delta[0, 0] = total.astype(BF16)

        def copy_c(dy):
            return remote(delta.at[0, dy], delta.at[1, dy], sem_es.at[i, dy], sem_er.at[i, dy], core_peer)

        for dy in order:
            back = NY - dy
            begin(remote(delta.at[0, 0], delta.at[0, back], sem_ds.at[i, dy], sem_dr.at[i, back], y_peer(dy)))
        begin(copy_c(0))
        yield
        for dy in nearest:
            remote(
                delta.at[0, 0], delta.at[0, dy], sem_ds.at[i, dy], sem_dr.at[i, dy], y_peer(dy)
            ).wait_recv()
            begin(copy_c(dy))
        yield
        for dy in range(NY):
            copy_c(dy).wait_recv()
        for part in range(2):
            half = core if part == 0 else 1 - core
            for dy in range(NY):
                added = delta[part, dy].astype(F32)
                if first:
                    total_out[quarter_rows(half, dy), :] = added
                else:
                    total_out[quarter_rows(half, dy), :] += added

    with jax.named_scope("qkv_products"):
        width1 = 3 * INNER
        states = hid[:, :COLS]
        normed = (states * gains[0:1, :]).astype(BF16)
        inward[0].wait()
        for j in range(3):
            own1[:, j * INNER : (j + 1) * INNER] = dot(normed, wqkv[j])
        own1[:, width1:] = square_sums(states)
        early[0].wait_recv()
        swap = remote(near_hid.at[my_half], near_hid.at[my_half], sem_ws.at[8], sem_wr.at[8], core_peer)
        begin(swap)
        remote(near_hid.at[my_half], near_hid.at[its_half], sem_ws.at[8], sem_wr.at[8], core_peer).wait_recv()
        early[1].wait_recv()
        states = near_hid[...]
        hid[:, COLS:] = states
        normed = (states * near_gain[0:1, :]).astype(BF16)
        own1[:, width1:] += square_sums(states)
        early[2].wait_recv()
        early[3].wait_recv()
        for j in range(3):
            own1[:, j * INNER : (j + 1) * INNER] += dot(normed, far_wqkv[j])

    with jax.named_scope("qkv_sums"):
        scatter_start(0, width1, BLK, zs1, zr1, own1)
        late_start()
        total, scale = scatter_end(0, width1, BLK, zs1, zr1, own1)
        qkv = (total * scale).astype(BF16)

    spread_heads = decode_heads()
    tokens = 2 * memory.shape[1]
    pairs = []

    def token_pairs():
        low_lane = iota((tokens, LANES), 1) < 64
        one = jnp.where(low_lane, 1.0, 0.0)
        for p in range(INNER // LANES):
            cols = slice(p * LANES, (p + 1) * LANES)
            k, v = (
                jnp.concatenate([memory[kv, :, cols], far_memory[kv, :, cols]], axis=0).astype(F32)
                for kv in range(2)
            )
            k2 = jnp.concatenate([jnp.where(low_lane, k, 0.0), jnp.where(low_lane, 0.0, k)], axis=0)
            v2 = jnp.concatenate(
                [
                    jnp.concatenate([jnp.where(low_lane, v, 0.0), one], axis=1),
                    jnp.concatenate([jnp.where(low_lane, 0.0, v), 1.0 - one], axis=1),
                ],
                axis=0,
            )
            pairs.append((k2.astype(BF16), v2.astype(BF16)))

    def pair_columns(t):
        return pair_copy(9 + t, last_s.at[t], last_r.at[t], pair_peer)

    def stream(t):
        gather_start(t, att.at[t])
        yield
        rows = gather_end(t, att.at[t])
        if t == 0:
            inward[1].wait()
            late[0].wait_recv()
        prod[t, :, :COLS] = dot(rows, wso[...])
        prod[t, :, COLS:] = dot(rows, far_wso[...])
        yield from head_sums(
            t, True, prod.at[t], summed.at[t], core_s.at[t], core_r.at[t], ys.at[t], yr.at[t], delta.at[t],
            lambda: cache_start(0) if t else None,
        )

        states = summed[t] + jnp.concatenate(
            [hid[dz * BLK + t * RB : dz * BLK + (t + 1) * RB, :] for dz in range(NZ)], axis=0
        )
        gain = jnp.concatenate([gains[1:2, :], near_gain[1:2, :]], axis=1)
        normed = (states * gain).astype(BF16)
        if t == 0:
            inward[2].wait()
            late[1].wait_recv()
        own = own2.at[t]
        own[:, :INNER] = dot(normed[:, :COLS], wcq[...]) + dot(normed[:, COLS:], far_wcq[...])
        own[:, INNER:] = square_sums(states)
        scatter_start(1 + t, INNER, RB, zs2.at[t], zr2.at[t], own)
        if t == 0:
            inward[3].wait()
            late[2].wait_recv()
            token_pairs()
        yield
        total, scale = scatter_end(1 + t, INNER, RB, zs2.at[t], zr2.at[t], own)
        query[t, 0] = ((total * scale).astype(BF16).astype(F32) * 0.125).astype(BF16)
        gather_start(2 + t, query.at[t])
        yield
        queries = gather_end(2 + t, query.at[t])
        low_out = iota((STREAM, LANES), 1) < 64
        accs, lses = [], []
        for p, (k2, v2) in enumerate(pairs):
            cols = slice(p * LANES, (p + 1) * LANES)
            scores = dot_t(queries[:, cols], k2)
            peak0 = jnp.max(scores[:, :tokens], axis=1, keepdims=True)
            peak1 = jnp.max(scores[:, tokens:], axis=1, keepdims=True)
            weights = jnp.concatenate(
                [jnp.exp(scores[:, :tokens] - peak0), jnp.exp(scores[:, tokens:] - peak1)], axis=1
            )
            both = dot(weights.astype(BF16), v2)
            lses.append(jnp.where(low_out, peak0, peak1) + jnp.log(both[:, LANES:]))
            acc = both[:, :LANES] / both[:, LANES:]
            accs.append(acc[:RB])
            narrow = acc.astype(BF16)
            for dz in range(1, NZ):
                zs3[t, dz - 1, :, cols] = narrow[dz * RB : (dz + 1) * RB]
        code = head_codes(lses)
        for dz in range(1, NZ):
            zs3[t, dz - 1, :, INNER:] = code[dz * RB : (dz + 1) * RB]
        for dz in far_first:
            begin(z_copy(3 + t, zs3.at[t], zr3.at[t], dz))
        yield
        peak = jnp.concatenate([lse[:RB] for lse in lses], axis=1)
        parts = [(jnp.concatenate(accs, axis=1), peak)]
        for dz in far_first[::-1]:
            z_copy(3 + t, zs3.at[t], zr3.at[t], dz).wait_recv()
            arrived = zr3[t, dz - 1]
            parts.append((arrived[:, :INNER].astype(F32), dot(arrived[:, INNER:], spread_heads)))
            peak = jnp.maximum(peak, parts[-1][1])
        weights = [jnp.exp(lse - peak) for _, lse in parts]
        acc, whole = parts[0][0] * weights[0], weights[0]
        for (a, _), w in zip(parts[1:], weights[1:]):
            acc += a * w
            whole += w
        mixed[t, 0] = (acc / whole).astype(BF16)
        gather_start(4 + t, mixed.at[t])
        yield
        rows = gather_end(4 + t, mixed.at[t])
        if t == 0:
            inward[4].wait()
            late[3].wait_recv()
        prod[t, :, :COLS] = dot(rows, wco[...])
        prod[t, :, COLS:] = dot(rows, far_wco[...])
        yield from head_sums(
            2 + t, False, prod.at[t], summed.at[t], core_s2.at[t], core_r2.at[t], ys2.at[t], yr2.at[t], delta2.at[t],
            lambda: cache_start(1) if t else None,
        )

        last_s[t] = summed[t, :, COLS:].astype(BF16)
        begin(pair_columns(t))
        for dz in range(NZ):
            out[t, rows_at(0, dz), :] = summed[t, dz * RB : (dz + 1) * RB, :COLS]

    streams = [stream(t) for t in range(2)]

    def ask_copy(o):
        return remote(ask_send.at[o], ask_recv.at[o], sem_as.at[o], sem_ar.at[o], back_peer(o))

    def reply_copy(o):
        return remote(reply_send.at[o], reply_recv.at[o], sem_rs.at[o], sem_rr.at[o], all_peer(o))

    def grown_copy(kv, o):
        return remote(
            grown_send.at[kv, o], grown_recv.at[kv, o], sem_ks.at[kv, o], sem_kr.at[kv, o], all_peer(o)
        )

    def side_by_side(rows, first, count):
        return jnp.concatenate([rows[(first + p) * RB : (first + p + 1) * RB] for p in range(count)], axis=1)

    def stacked(rows):
        return [rows[:, p * LANES : (p + 1) * LANES] for p in range(rows.shape[1] // LANES)]

    def entry(t, kv):
        return qkv[t * RB : (t + 1) * RB, (1 + kv) * INNER : (2 + kv) * INNER]

    messages = (NALL, SLOTS * KP, LANES)
    flat = (NALL * SLOTS * KP, LANES)
    queries_of = [
        (qkv[t * RB : (t + 1) * RB, :INNER].astype(F32) * 0.125).astype(BF16) for t in range(2)
    ]
    with jax.named_scope("query_send"):
        send1, recv1 = picks(parents[1:2, :], x, z, beam)
        four = stacked(queries_of[1])
        asked = jnp.concatenate(four + four, axis=0)
        ask_send[...] = dot(spread_matrix(recv1, KP), asked).astype(BF16).reshape(messages)
        ask_recv[0] = ask_send[0]
        for o in range(1, NALL):
            begin(ask_copy(o))

    with jax.named_scope("parent_attention"):
        same_head = (iota((INNER, INNER), 0) >> 6) == (iota((INNER, INNER), 1) >> 6)
        ones = jnp.where(same_head, 1.0, 0.0).astype(BF16)
        of_head = jnp.where((iota((8, INNER), 1) >> 6) == iota((8, INNER), 0), 1.0, 0.0).astype(BF16)
        wide_bias = sum(
            lax.dot_general(part.astype(BF16), of_head, (((0,), (0,)), ((), ())), preferred_element_type=F32)
            for part in split3(bias[...])
        )
        pick = gather_matrix(recv0, CP)
        for o in range(1, NALL):
            hop_copy(o).wait_recv()
        held0 = dot(pick, hop_recv[...].reshape(NALL * SLOTS * CP, COLS)).astype(BF16)
        grown0 = [
            [side_by_side(held0, (kv * PREV + pos) * 2, 2) for pos in range(PREV)] + [entry(0, kv)] for kv in range(2)
        ]
        acc, _, whole = attend(
            queries_of[0].astype(F32), *grown0,
            [wide_bias[PREV - j : PREV - j + 1, :] for j in range(PREV + 1)], ones,
        )
        att[0, 0] = (acc / whole).astype(BF16)
        next(streams[0])
        copies = [[dot(send1, rows) for rows in side] for side in grown0]
        rows_of_piece = [piece_rows(p) for p in range(5)]
        back = jnp.concatenate(rows_of_piece, axis=0)
        for o in range(1, NALL):
            ask_copy(o).wait_recv()
        arrived = ask_recv[...].reshape(flat)
        q = jnp.concatenate([dot(rows_of_piece[p], arrived) for p in range(4)], axis=1)
        last = PREV + 1
        acc, peak, whole = attend(
            q, *copies, [wide_bias[last - j : last - j + 1, :] for j in range(last)], ones
        )
        mine = (acc / whole).astype(BF16)
        lse = peak + jnp.log(whole)
        code = head_codes(stacked(lse))
        turned = lax.dot_general(
            back, jnp.concatenate(stacked(mine) + [code], axis=0), (((0,), (0,)), ((), ())), preferred_element_type=F32
        )
        reply_send[...] = turned.astype(BF16).reshape(messages)
        reply_recv[0] = reply_send[0]
        for o in range(1, NALL):
            begin(reply_copy(o))

    with jax.named_scope("self_attention"):
        pick1 = gather_matrix(recv1, KP)
        next(streams[0])
        fresh = queries_of[1].astype(F32) * entry(1, 0).astype(F32)
        high = fresh.astype(BF16)
        low = (fresh - high.astype(F32)).astype(BF16)
        score = dot(high, ones) + dot(low, ones) + wide_bias[0:1, :]
        next(streams[0])
        for o in range(1, NALL):
            reply_copy(o).wait_recv()
        replies = dot(pick1, reply_recv[...].reshape(flat)).astype(BF16)
        lse = dot(replies[4 * RB : 5 * RB], spread_heads)
        peak = jnp.maximum(lse, score)
        w_old, w_new = jnp.exp(lse - peak), jnp.exp(score - peak)
        acc = side_by_side(replies, 0, 4).astype(F32) * w_old + w_new * entry(1, 1).astype(F32)
        att[1, 0] = (acc / (w_old + w_new)).astype(BF16)
        next(streams[1])

    def cache_ready():
        spread = spread_matrix(send1, GP)
        for kv in range(2):
            new = entry(0, kv)
            halves = [new[:, :COLS], new[:, COLS:]]
            first = kv * PREV * 2 * RB
            rows = jnp.concatenate([held0[first : first + PREV * 2 * RB], *halves, *halves], axis=0)
            grown_send[kv] = dot(spread, rows).astype(BF16).reshape(NALL, SLOTS * GP, COLS)
            grown_recv[kv, 0] = grown_send[kv, 0]

    def cache_start(kv):
        for o in range(1, NALL):
            begin(grown_copy(kv, o))

    def cache_end():
        pick = gather_matrix(recv1, GP)
        place = iota((RB * (PREV + 2), RB * (PREV + 2)), 0)
        from_row = (place & 7) * RB + (place >> 3)
        turn = jnp.where(from_row == iota(place.shape, 1), 1.0, 0.0).astype(BF16)
        for kv in range(2):
            for o in range(1, NALL):
                grown_copy(kv, o).wait_recv()
            held1 = dot(pick, grown_recv[kv].reshape(NALL * SLOTS * GP, COLS)).astype(BF16)
            side = [side_by_side(held1, pos * 2, 2) for pos in range(PREV + 1)] + [entry(1, kv)]
            cache_out[kv] = dot(turn, jnp.concatenate(side, axis=0)).astype(BF16)

    cache_ready()
    running = list(streams)
    while running:
        running = [stream for stream in running if next(stream, "end") != "end"]
    cache_end()
    for t in range(2):
        pair_columns(t).wait_recv()
        for dz in range(NZ):
            out[t, rows_at(1, dz), :] = last_r[t, dz * RB : (dz + 1) * RB, :].astype(F32)
    for copy in pending:
        copy.wait_send()


def body(
    hidden_in, norm_gains, w_qkv, w_self_out, w_cross_q, w_cross_out, pos_bias, self_cache, memory, parents
):
    dma = pltpu.SemaphoreType.DMA
    wide1, wide2 = 3 * INNER + LANES, INNER + LANES
    part = STREAM // 2
    half_pair = [pltpu.VMEM((2, part, WIDE), BF16)] * 2
    quarters = [pltpu.VMEM((2, NY - 1, part // NY, WIDE), BF16)] * 2
    head_buffers = [*half_pair, *quarters, pltpu.VMEM((2, 2, NY, part // NY, WIDE), BF16)]
    in_vmem = pl.BlockSpec(memory_space=pltpu.VMEM)
    in_hbm = pl.BlockSpec(memory_space=pl.ANY)
    added, cache_rows = pl.pallas_call(
        kernel,
        out_shape=(
            jax.ShapeDtypeStruct(hidden_in.shape, F32),
            jax.ShapeDtypeStruct((2, RB * (PREV + 2), INNER), BF16),
        ),
        in_specs=[in_vmem] * 2 + [in_hbm] * 4 + [in_vmem] * 2 + [in_hbm, in_vmem],
        out_specs=(in_vmem, in_vmem),
        scratch_shapes=[
            pltpu.VMEM((3, COLS, INNER), BF16),
            pltpu.VMEM(w_self_out.shape, BF16),
            pltpu.VMEM(w_cross_q.shape, BF16),
            pltpu.VMEM(w_cross_out.shape, BF16),
            pltpu.VMEM(memory.shape, BF16),
            pltpu.VMEM((ROWS, COLS), F32),
            pltpu.VMEM((ROWS, COLS), F32),
            pltpu.VMEM((8, COLS), F32),
            pltpu.VMEM((8, COLS), F32),
            pltpu.VMEM((3, COLS, INNER), BF16),
            pltpu.VMEM(w_self_out.shape, BF16),
            pltpu.VMEM(w_cross_q.shape, BF16),
            pltpu.VMEM(w_cross_out.shape, BF16),
            pltpu.VMEM(memory.shape, BF16),
            pltpu.VMEM((ROWS, WIDE), F32),
            *[pltpu.VMEM((2, STREAM, WIDE), F32)] * 2,
            *[pltpu.VMEM((NZ - 1, BLK, wide1), BF16)] * 2,
            pltpu.VMEM((ROWS, wide1), F32),
            *[pltpu.VMEM((2, NZ - 1, RB, wide2), BF16)] * 2,
            pltpu.VMEM((2, STREAM, wide2), F32),
            *[pltpu.VMEM((2, NZ - 1, RB, wide2), BF16)] * 2,
            *[pltpu.VMEM((NALL, SLOTS * CP, COLS), BF16)] * 2,
            *[pltpu.VMEM((2, NALL, SLOTS * GP, COLS), BF16)] * 2,
            *[pltpu.VMEM((NALL, SLOTS * KP, LANES), BF16)] * 4,
            *[pltpu.VMEM((2, NZ, RB, INNER), BF16)] * 3,
            *[pltpu.VMEM((2, STREAM, COLS), BF16)] * 2,
            *head_buffers,
            *head_buffers,
            dma((11,)), dma((11,)), dma((5, NZ - 1)), dma((5, NZ - 1)),
            dma((NALL,)), dma((NALL,)), dma((2, NALL)), dma((2, NALL)),
            dma((6, NZ)), dma((6, NZ)),
            dma((4,)), dma((4,)), dma((4, NY - 1)), dma((4, NY - 1)),
            dma((4, NY)), dma((4, NY)), dma((4, NY)), dma((4, NY)),
            dma((NALL,)), dma((NALL,)), dma((NALL,)), dma((NALL,)), dma((5,)),
        ],
        compiler_params=pltpu.CompilerParams(
            collective_id=0, has_side_effects=True, vmem_limit_bytes=58 * 1024 * 1024
        ),
        name="decode",
    )(
        hidden_in, norm_gains, w_qkv.transpose(1, 0, 2), w_self_out, w_cross_q, w_cross_out, pos_bias,
        self_cache[:, 0].transpose(0, 2, 1, 3), memory, parents,
    )
    return hidden_in + added, cache_rows.reshape(2, 1, RB, PREV + 2, INNER)


def solution(mesh):
    placed = (
        P(None, "beam", "blk"),
        P(None, "blk"),
        P("blk", None, "head"),
        P("head", "blk"),
        P("blk", "head"),
        P("head", "blk"),
        P("head", None),
        P(None, "beam", "blk", None, "head"),
        P(None, "blk", "head"),
        P(),
    )
    return jax.shard_map(
        body,
        mesh=mesh,
        in_specs=placed,
        out_specs=(P(None, "beam", "blk"), P(None, "beam", "blk", None, "head")),
        check_vma=False,
    )
```

```python
import jax
import jax.numpy as jnp
from jax import lax
from jax.experimental import pallas as pl
from jax.experimental.pallas import tpu as pltpu
from jax.sharding import PartitionSpec as P

D = 4096
EPS = 1e-06
MESH = pl.DeviceIdType.MESH
F32, BF16 = jnp.float32, jnp.bfloat16
NZ, NX, NB = 8, 2, 2
NBLK, NALL = NZ * NX, NZ * NX * NB
NY, NC = 4, 2
RB = 16
BLK = 2 * RB
ROWS = NZ * BLK
HALF = ROWS // 2
INNER = 512
COLS = 256
WIDE = 2 * COLS
SPLIT = 144
PREV = 6
CP = 2 * PREV * 2
KP = 8
GP = 16
LANES = 128
SLOTS = 2


def dot(a, b):
    return jnp.dot(a, b, preferred_element_type=F32)


def dot_t(a, b):
    return lax.dot_general(a, b, (((1,), (1,)), ((), ())), preferred_element_type=F32)


def iota(shape, dim):
    return lax.broadcasted_iota(jnp.int32, shape, dim)


def split3(x):
    high = x.astype(BF16).astype(F32)
    middle = (x - high).astype(BF16).astype(F32)
    return high, middle, x - high - middle


def encode(x):
    high, middle, low = split3(x)
    place = iota(x.shape, 1) & 15
    return jnp.where(place < 4, high, jnp.where(place < 8, middle, low)).astype(BF16)


def part_weight(place, lanes):
    return jnp.where(place < 8, 4.0 / lanes, 2.0 / lanes)


def decode_row():
    lane = iota((LANES, LANES), 0)
    return part_weight(lane & 15, LANES).astype(BF16)


def decode_heads():
    lane, col = iota((LANES, INNER), 0), iota((LANES, INNER), 1)
    same = ((lane >> 6) == ((col >> 6) & 1)) & (((lane >> 4) & 3) == (col >> 7))
    return jnp.where(same, part_weight(lane & 15, 16), 0.0).astype(BF16)


def piece_mask(shape, dim, pieces):
    place = (iota(shape, dim).astype(F32) + 0.5) * (1.0 / pieces)
    piece = (place - jnp.floor(place)) * pieces - 0.5
    return jnp.abs(piece - (iota(shape, 1 - dim) >> 4).astype(F32)) < 0.25


def slot_matrix(shape, dim, pieces):
    q = iota(shape, 1 - dim)
    first = ((q & (NALL - 1)) * SLOTS + (q >> 5)) * pieces
    place = iota(shape, dim)
    return jnp.where((place >= first) & (place < first + pieces), 1.0, 0.0).astype(BF16)


def spread_matrix(chosen, pieces):
    rows, cols = NALL * SLOTS * pieces, RB * pieces
    repeat = jnp.where((iota((RB, cols), 1) & 15) == iota((RB, cols), 0), 1.0, 0.0).astype(BF16)
    full = dot(slot_matrix((rows, NALL * SLOTS), 0, pieces), dot(chosen, repeat).astype(BF16))
    return jnp.where(piece_mask((rows, cols), 0, pieces), full, 0.0).astype(BF16)


def gather_matrix(chosen, pieces):
    rows, cols = RB * pieces, NALL * SLOTS * pieces
    repeat = jnp.where((iota((rows, RB), 0) & 15) == iota((rows, RB), 1), 1.0, 0.0).astype(BF16)
    full = dot(dot_t(repeat, chosen).astype(BF16), slot_matrix((NALL * SLOTS, cols), 1, pieces))
    return jnp.where(piece_mask((rows, cols), 1, pieces), full, 0.0).astype(BF16)


def piece_rows(p):
    q = iota((NALL * SLOTS, NALL * SLOTS * KP), 0)
    row = ((q & (NALL - 1)) * SLOTS + (q >> 5)) * KP + p
    return jnp.where(iota(q.shape, 1) == row, 1.0, 0.0).astype(BF16)


def head_codes(four):
    group = (iota(four[0].shape, 1) >> 4) & 3
    low_pair, high_pair = jnp.where(group == 0, four[0], four[1]), jnp.where(group == 2, four[2], four[3])
    return encode(jnp.where(group < 2, low_pair, high_pair))


def attend(q, keys, values, biases, ones):
    rows = q.shape[0]
    products = jnp.concatenate([q * k.astype(F32) for k in keys], axis=0)
    high = products.astype(BF16)
    low = (products - high.astype(F32)).astype(BF16)
    sums = dot(high, ones) + dot(low, ones)
    scores = [sums[j * rows : (j + 1) * rows] + b for j, b in enumerate(biases)]
    peak = scores[0]
    for s in scores[1:]:
        peak = jnp.maximum(peak, s)
    weights = [jnp.exp(s - peak) for s in scores]
    whole, acc = weights[0], weights[0].astype(BF16).astype(F32) * values[0].astype(F32)
    for w, v in zip(weights[1:], values[1:]):
        whole += w
        acc += w.astype(BF16).astype(F32) * v.astype(F32)
    return acc, peak, whole


def picks(parents, x, z, beam):
    square = (NALL, NALL)
    o, block = iota(square, 0), iota(square, 1)
    flip_x, flip_b = (o >> 3) & 1, o >> 4
    at_offset = (beam + flip_b - 2 * beam * flip_b) * NBLK + (x + flip_x - 2 * x * flip_x) * NZ + ((z + o) & 7)
    permute = jnp.where(at_offset == block, 1.0, 0.0).astype(BF16)
    wide = (NALL, NALL * RB)
    in_block = (iota(wide, 1) >> 4) == iota(wide, 0)
    fold = jnp.where((iota(wide[::-1][:1] + (RB,), 0) & 15) == iota(wide[::-1][:1] + (RB,), 1), 1.0, 0.0).astype(BF16)

    def folded(row):
        blocks = dot(jnp.where(in_block, row.astype(F32), 0.0).astype(BF16), fold)
        return dot(permute, blocks.astype(BF16))

    source, local = folded(parents >> 4), folded(parents & 15)
    lane = iota((NALL, RB), 1)
    slot = jnp.zeros((NALL, RB), F32)
    for k in range(RB - 1):
        slot += jnp.where((source[:, k : k + 1] == source) & (lane > k), 1.0, 0.0)
    me = (beam * NBLK + x * NZ + z).astype(F32)
    send = []
    for s in range(SLOTS):
        mine = jnp.where((source == me) & (slot == s), local, -1.0)
        send.append(sum(jnp.where(mine[:, k : k + 1] == lane.astype(F32), 1.0, 0.0) for k in range(RB)))
    own = source[:1].astype(jnp.int32)
    own_b, own_x, own_z = own >> 4, (own >> 3) & 1, own & 7
    differ_b, differ_x = jnp.abs(own_b - beam), jnp.abs(own_x - x)
    offset = differ_b * NBLK + differ_x * NZ + ((z - own_z + NZ) & 7) + slot[:1].astype(jnp.int32) * NALL
    q = iota((NALL * SLOTS, RB), 0)
    recv = jnp.where(q == offset, 1.0, 0.0)
    return jnp.concatenate(send, axis=0).astype(BF16), recv.astype(BF16)


def kernel(
    hidden, gains, wqkv_hbm, wso_hbm, wcq_hbm, wco_hbm, bias, cache, memory_hbm, parents,
    out, cache_out,
    wqkv, wso, wcq, wco, memory,
    far_hid, near_hid, far_gain, near_gain, far_wqkv, far_wso, far_wcq, far_wco, far_memory,
    hid, summed, prod, zs1, zr1, own1, zs2, zr2, own2, zs3, zr3,
    hop_send, hop_recv, grown_send, grown_recv, ask_send, ask_recv, reply_send, reply_recv, att, query, mixed, last_s, last_r,
    core_s, core_r, ys, yr, delta, core_s2, core_r2, ys2, yr2, delta2,
    sem_ws, sem_wr, sem_zs, sem_zr, sem_hs, sem_hr, sem_ks, sem_kr, sem_gs, sem_gr,
    sem_cs, sem_cr, sem_ys, sem_yr, sem_ds, sem_dr, sem_es, sem_er, sem_as, sem_ar, sem_rs, sem_rr, sem_in,
):
    blk, beam, head = lax.axis_index("blk"), lax.axis_index("beam"), lax.axis_index("head")
    x, z = blk // NZ, lax.rem(blk, NZ)
    y, core = head // NC, lax.rem(head, NC)

    def block_at(dx, dz):
        return (x if dx == 0 else 1 - x) * NZ + lax.rem(z + dz, NZ)

    def z_peer(dz):
        return {"blk": block_at(0, dz)}

    def all_peer(o):
        where = {"blk": block_at((o // NZ) % NX, o % NZ)}
        if o >= NBLK:
            where["beam"] = 1 - beam
        return where

    def back_peer(o):
        where = {"blk": block_at((o // NZ) % NX, (NZ - o) % NZ)}
        if o >= NBLK:
            where["beam"] = 1 - beam
        return where

    pair_peer = all_peer(NZ)
    other_peer = all_peer(NBLK + NZ)
    core_peer = {"head": y * NC + 1 - core}

    def y_peer(dy):
        return {"head": lax.rem(y + dy, NY) * NC + core}

    def remote(src, dst, send, recv, peer):
        return pltpu.make_async_remote_copy(
            src, dst, send, recv, device_id=peer, device_id_type=MESH
        )

    def rows_at(dx, dz):
        return pl.ds(pl.multiple_of(block_at(dx, dz) * RB, RB), RB)

    with jax.named_scope("entry_barrier"):
        barrier = pltpu.get_barrier_semaphore()
        peers = [all_peer(o) for o in range(1, NALL)]
        peers += [core_peer] + [y_peer(dy) for dy in range(1, NY)]
        for peer in peers:
            pl.semaphore_signal(barrier, inc=1, device_id=peer, device_id_type=MESH)
        inward = [
            pltpu.make_async_copy(src, dst, sem_in.at[i])
            for i, (src, dst) in enumerate(
                ((wqkv_hbm, wqkv), (wso_hbm, wso), (wcq_hbm, wcq), (memory_hbm, memory), (wco_hbm, wco))
            )
        ]
        for copy in inward:
            copy.start()
        for dz in range(NZ):
            for t in range(2):
                rows = slice(dz * BLK + t * RB, dz * BLK + (t + 1) * RB)
                far_hid[rows, :] = hidden[t, rows_at(1, dz), :]
                hid[rows, :COLS] = hidden[t, rows_at(0, dz), :]
        far_gain[...] = jnp.zeros_like(far_gain)
        far_gain[:2, :] = gains[...]

    with jax.named_scope("own_products"):
        send0, recv0 = picks(parents[0:1, :], x, z, beam)
        pieces = [
            cache[kv, pos, :, c * COLS : (c + 1) * COLS] for kv in range(2) for pos in range(PREV) for c in range(2)
        ]
        picked = dot(spread_matrix(send0, CP), jnp.concatenate(pieces, axis=0)).astype(BF16)
        hop_send[...] = picked.reshape(NALL, SLOTS * CP, COLS)
        hop_recv[0] = hop_send[0]
        pl.semaphore_wait(barrier, len(peers))

    pending = []

    def begin(copy):
        copy.start()
        pending.append(copy)

    my_half = pl.ds(pl.multiple_of(core * HALF, HALF), HALF)
    its_half = pl.ds(pl.multiple_of((1 - core) * HALF, HALF), HALF)

    def pair_copy(i, src, dst, peer):
        return remote(src, dst, sem_ws.at[i], sem_wr.at[i], peer)

    early = [
        pair_copy(0, far_hid.at[my_half], near_hid.at[my_half], pair_peer),
        pair_copy(1, far_gain, near_gain, pair_peer),
        pair_copy(2, wqkv_hbm.at[:, pl.ds(0, SPLIT)], far_wqkv.at[:, pl.ds(0, SPLIT)], other_peer),
        pair_copy(3, wqkv_hbm.at[:, pl.ds(SPLIT, COLS - SPLIT)], far_wqkv.at[:, pl.ds(SPLIT, COLS - SPLIT)], pair_peer),
    ]
    late = [
        pair_copy(4, wso_hbm, far_wso, other_peer),
        pair_copy(5, wcq_hbm, far_wcq, pair_peer),
        pair_copy(6, memory_hbm, far_memory, other_peer),
        pair_copy(7, wco_hbm, far_wco, pair_peer),
    ]
    for copy in early:
        begin(copy)

    def hop_copy(o):
        return remote(hop_send.at[o], hop_recv.at[o], sem_hs.at[o], sem_hr.at[o], all_peer(o))

    with jax.named_scope("cache_send"):
        for o in range(1, NALL):
            begin(hop_copy(o))

    def z_copy(phase, zs, zr, dz):
        return remote(
            zs.at[dz - 1], zr.at[dz - 1], sem_zs.at[phase, dz - 1], sem_zr.at[phase, dz - 1], z_peer(dz)
        )

    far_first = (4, 3, 5, 2, 6, 1, 7)

    def late_start():
        for copy in late:
            begin(copy)

    def scatter_sums(phase, width, zs, zr, own, meanwhile=None):
        for dz in far_first:
            rows = slice(dz * BLK, (dz + 1) * BLK)
            zs[dz - 1, :, :width] = own[rows, :width].astype(BF16)
            zs[dz - 1, :, width:] = encode(own[rows, width:])
            begin(z_copy(phase, zs, zr, dz))
        if meanwhile:
            meanwhile()
        total, squares = own[:BLK, :width], own[:BLK, width:]
        for dz in far_first[::-1]:
            z_copy(phase, zs, zr, dz).wait_recv()
            arrived = zr[dz - 1]
            total += arrived[:, :width].astype(F32)
            squares += dot(arrived[:, width:], decode_row())
        return total, lax.rsqrt(squares[:, :1] / D + EPS)

    def square_sums(states):
        return jnp.broadcast_to(jnp.sum(states * states, axis=1, keepdims=True), (ROWS, LANES))

    def gather_rows(phase, blocks, meanwhile=None):
        def copy(dz):
            back = NZ - dz
            return remote(
                blocks.at[0], blocks.at[back], sem_gs.at[phase, dz], sem_gr.at[phase, back], z_peer(dz)
            )

        for dz in far_first:
            begin(copy(dz))
        if meanwhile:
            meanwhile()
        for dz in far_first[::-1]:
            remote(
                blocks.at[0], blocks.at[dz], sem_gs.at[phase, dz], sem_gr.at[phase, dz], z_peer(dz)
            ).wait_recv()
        return blocks[...].reshape(ROWS, INNER)

    quarter = HALF // NY

    def quarter_rows(half, dy):
        start = half * HALF + lax.rem(y + dy, NY) * quarter
        return pl.ds(pl.multiple_of(start, quarter), quarter)

    def head_sums(phase, core_s, core_r, ys, yr, delta, meanwhile=None):
        core_s[...] = prod[its_half, :].astype(BF16)
        copy = remote(core_s, core_r, sem_cs.at[phase], sem_cr.at[phase], core_peer)
        begin(copy)
        copy.wait_recv()
        prod[my_half, :] += core_r[...].astype(F32)

        def copy_sum(dy):
            return remote(
                ys.at[dy - 1], yr.at[dy - 1], sem_ys.at[phase, dy - 1], sem_yr.at[phase, dy - 1], y_peer(dy)
            )

        order = (2, 1, 3)
        for dy in order:
            ys[dy - 1] = prod[quarter_rows(core, dy), :].astype(BF16)
            begin(copy_sum(dy))
        if meanwhile:
            meanwhile()
        total = prod[quarter_rows(core, 0), :]
        for dy in (1, 3, 2):
            copy_sum(dy).wait_recv()
            total += yr[dy - 1].astype(F32)
        delta[0, 0] = total.astype(BF16)

        def copy_y(dy):
            back = NY - dy
            return remote(
                delta.at[0, 0], delta.at[0, back], sem_ds.at[phase, dy], sem_dr.at[phase, back], y_peer(dy)
            )

        def copy_c(dy):
            return remote(
                delta.at[0, dy], delta.at[1, dy], sem_es.at[phase, dy], sem_er.at[phase, dy], core_peer
            )

        for dy in order:
            begin(copy_y(dy))
        begin(copy_c(0))
        for dy in (1, 3, 2):
            remote(
                delta.at[0, 0], delta.at[0, dy], sem_ds.at[phase, dy], sem_dr.at[phase, dy], y_peer(dy)
            ).wait_recv()
            begin(copy_c(dy))
        for dy in range(NY):
            copy_c(dy).wait_recv()
        for part in range(2):
            half = core if part == 0 else 1 - core
            for dy in range(NY):
                added = delta[part, dy].astype(F32)
                if phase == 0:
                    hid[quarter_rows(half, dy), :] += added
                    summed[quarter_rows(half, dy), :] = added
                else:
                    summed[quarter_rows(half, dy), :] += added

    with jax.named_scope("qkv_products"):
        width1 = 3 * INNER
        states = hid[:, :COLS]
        normed = (states * gains[0:1, :]).astype(BF16)
        inward[0].wait()
        for j in range(3):
            own1[:, j * INNER : (j + 1) * INNER] = dot(normed, wqkv[j])
        own1[:, width1:] = square_sums(states)
        early[0].wait_recv()
        swap = remote(near_hid.at[my_half], near_hid.at[my_half], sem_ws.at[8], sem_wr.at[8], core_peer)
        begin(swap)
        remote(near_hid.at[my_half], near_hid.at[its_half], sem_ws.at[8], sem_wr.at[8], core_peer).wait_recv()
        early[1].wait_recv()
        states = near_hid[...]
        hid[:, COLS:] = states
        normed = (states * near_gain[0:1, :]).astype(BF16)
        own1[:, width1:] += square_sums(states)
        early[2].wait_recv()
        early[3].wait_recv()
        for j in range(3):
            own1[:, j * INNER : (j + 1) * INNER] += dot(normed, far_wqkv[j])

    with jax.named_scope("qkv_sums"):
        total, scale = scatter_sums(0, width1, zs1, zr1, own1, late_start)
        qkv = (total * scale).astype(BF16)

    def ask_copy(o):
        return remote(ask_send.at[o], ask_recv.at[o], sem_as.at[o], sem_ar.at[o], back_peer(o))

    def reply_copy(o):
        return remote(reply_send.at[o], reply_recv.at[o], sem_rs.at[o], sem_rr.at[o], all_peer(o))

    def grown_copy(kv, o):
        return remote(
            grown_send.at[kv, o], grown_recv.at[kv, o], sem_ks.at[kv, o], sem_kr.at[kv, o], all_peer(o)
        )

    def side_by_side(rows, first, count):
        return jnp.concatenate([rows[(first + p) * RB : (first + p + 1) * RB] for p in range(count)], axis=1)

    def stacked(rows):
        return [rows[:, p * LANES : (p + 1) * LANES] for p in range(rows.shape[1] // LANES)]

    def entry(t, kv):
        return qkv[t * RB : (t + 1) * RB, (1 + kv) * INNER : (2 + kv) * INNER]

    messages = (NALL, SLOTS * KP, LANES)
    flat = (NALL * SLOTS * KP, LANES)
    queries_of = [
        (qkv[t * RB : (t + 1) * RB, :INNER].astype(F32) * 0.125).astype(BF16) for t in range(2)
    ]
    with jax.named_scope("query_send"):
        send1, recv1 = picks(parents[1:2, :], x, z, beam)
        four = stacked(queries_of[1])
        asked = jnp.concatenate(four + four, axis=0)
        ask_send[...] = dot(spread_matrix(recv1, KP), asked).astype(BF16).reshape(messages)
        ask_recv[0] = ask_send[0]
        for o in range(1, NALL):
            begin(ask_copy(o))

    with jax.named_scope("parent_attention"):
        same_head = (iota((INNER, INNER), 0) >> 6) == (iota((INNER, INNER), 1) >> 6)
        ones = jnp.where(same_head, 1.0, 0.0).astype(BF16)
        of_head = jnp.where((iota((8, INNER), 1) >> 6) == iota((8, INNER), 0), 1.0, 0.0).astype(BF16)
        wide_bias = sum(
            lax.dot_general(part.astype(BF16), of_head, (((0,), (0,)), ((), ())), preferred_element_type=F32)
            for part in split3(bias[...])
        )
        pick = gather_matrix(recv0, CP)
        for o in range(1, NALL):
            hop_copy(o).wait_recv()
        held0 = dot(pick, hop_recv[...].reshape(NALL * SLOTS * CP, COLS)).astype(BF16)
        grown0 = [
            [side_by_side(held0, (kv * PREV + pos) * 2, 2) for pos in range(PREV)] + [entry(0, kv)] for kv in range(2)
        ]
        copies = [[dot(send1, rows) for rows in side] for side in grown0]
        rows_of_piece = [piece_rows(p) for p in range(5)]
        back = jnp.concatenate(rows_of_piece, axis=0)
        for o in range(1, NALL):
            ask_copy(o).wait_recv()
        arrived = ask_recv[...].reshape(flat)
        q = jnp.concatenate([dot(rows_of_piece[p], arrived) for p in range(4)], axis=1)
        last = PREV + 1
        acc, peak, whole = attend(
            q, *copies, [wide_bias[last - j : last - j + 1, :] for j in range(last)], ones
        )
        mine = (acc / whole).astype(BF16)
        lse = peak + jnp.log(whole)
        code = head_codes(stacked(lse))
        turned = lax.dot_general(
            back, jnp.concatenate(stacked(mine) + [code], axis=0), (((0,), (0,)), ((), ())), preferred_element_type=F32
        )
        reply_send[...] = turned.astype(BF16).reshape(messages)
        reply_recv[0] = reply_send[0]
        for o in range(1, NALL):
            begin(reply_copy(o))

    with jax.named_scope("self_attention"):
        acc, _, whole = attend(
            queries_of[0].astype(F32), *grown0,
            [wide_bias[PREV - j : PREV - j + 1, :] for j in range(PREV + 1)], ones,
        )
        att[0, :RB, :] = (acc / whole).astype(BF16)
        pick1 = gather_matrix(recv1, KP)
        spread_heads = decode_heads()
        fresh = queries_of[1].astype(F32) * entry(1, 0).astype(F32)
        high = fresh.astype(BF16)
        low = (fresh - high.astype(F32)).astype(BF16)
        score = dot(high, ones) + dot(low, ones) + wide_bias[0:1, :]
        for o in range(1, NALL):
            reply_copy(o).wait_recv()
        replies = dot(pick1, reply_recv[...].reshape(flat)).astype(BF16)
        lse = dot(replies[4 * RB : 5 * RB], spread_heads)
        peak = jnp.maximum(lse, score)
        w_old, w_new = jnp.exp(lse - peak), jnp.exp(score - peak)
        acc = side_by_side(replies, 0, 4).astype(F32) * w_old + w_new * entry(1, 1).astype(F32)
        att[0, RB:, :] = (acc / (w_old + w_new)).astype(BF16)

    def cache_ready():
        spread = spread_matrix(send1, GP)
        for kv in range(2):
            new = entry(0, kv)
            halves = [new[:, :COLS], new[:, COLS:]]
            first = kv * PREV * 2 * RB
            rows = jnp.concatenate([held0[first : first + PREV * 2 * RB], *halves, *halves], axis=0)
            grown_send[kv] = dot(spread, rows).astype(BF16).reshape(NALL, SLOTS * GP, COLS)
            grown_recv[kv, 0] = grown_send[kv, 0]

    def cache_start(kv):
        for o in range(1, NALL):
            begin(grown_copy(kv, o))

    arrange = []

    def cache_end(kv):
        if not arrange:
            place = iota((RB * (PREV + 2), RB * (PREV + 2)), 0)
            from_row = (place & 7) * RB + (place >> 3)
            turn = jnp.where(from_row == iota(place.shape, 1), 1.0, 0.0).astype(BF16)
            arrange.extend((gather_matrix(recv1, GP), turn))
        pick, turn = arrange
        for o in range(1, NALL):
            grown_copy(kv, o).wait_recv()
        held1 = dot(pick, grown_recv[kv].reshape(NALL * SLOTS * GP, COLS)).astype(BF16)
        side = [side_by_side(held1, pos * 2, 2) for pos in range(PREV + 1)] + [entry(1, kv)]
        cache_out[kv] = dot(turn, jnp.concatenate(side, axis=0)).astype(BF16)

    with jax.named_scope("self_out"):
        rows = gather_rows(0, att, cache_ready)
        inward[1].wait()
        late[0].wait_recv()
        prod[:, :COLS] = dot(rows, wso[...])
        prod[:, COLS:] = dot(rows, far_wso[...])
        head_sums(0, core_s, core_r, ys, yr, delta, lambda: cache_start(0))

    with jax.named_scope("cross_query_products"):
        states = hid[...]
        gain = jnp.concatenate([gains[1:2, :], near_gain[1:2, :]], axis=1)
        normed = (states * gain).astype(BF16)
        inward[2].wait()
        late[1].wait_recv()
        own2[:, :INNER] = dot(normed[:, :COLS], wcq[...]) + dot(normed[:, COLS:], far_wcq[...])
        own2[:, INNER:] = square_sums(states)

    with jax.named_scope("cross_query_sums"):
        total, scale = scatter_sums(1, INNER, zs2, zr2, own2)
        query[0] = ((total * scale).astype(BF16).astype(F32) * 0.125).astype(BF16)

    with jax.named_scope("cross_query_gather"):
        queries = gather_rows(1, query)

    with jax.named_scope("cross_partial"):
        inward[3].wait()
        late[2].wait_recv()
        tokens = 2 * memory.shape[1]
        low_lane = iota((tokens, LANES), 1) < 64
        low_out = iota((ROWS, LANES), 1) < 64
        one = jnp.where(low_lane, 1.0, 0.0)
        accs, lses = [], []
        for p in range(INNER // LANES):
            cols = slice(p * LANES, (p + 1) * LANES)
            k, v = (
                jnp.concatenate([memory[kv, :, cols], far_memory[kv, :, cols]], axis=0).astype(F32)
                for kv in range(2)
            )
            k2 = jnp.concatenate([jnp.where(low_lane, k, 0.0), jnp.where(low_lane, 0.0, k)], axis=0)
            v2 = jnp.concatenate(
                [
                    jnp.concatenate([jnp.where(low_lane, v, 0.0), one], axis=1),
                    jnp.concatenate([jnp.where(low_lane, 0.0, v), 1.0 - one], axis=1),
                ],
                axis=0,
            )
            scores = dot_t(queries[:, cols], k2.astype(BF16))
            peak0 = jnp.max(scores[:, :tokens], axis=1, keepdims=True)
            peak1 = jnp.max(scores[:, tokens:], axis=1, keepdims=True)
            weights = jnp.concatenate(
                [jnp.exp(scores[:, :tokens] - peak0), jnp.exp(scores[:, tokens:] - peak1)], axis=1
            )
            both = dot(weights.astype(BF16), v2.astype(BF16))
            lses.append(jnp.where(low_out, peak0, peak1) + jnp.log(both[:, LANES:]))
            acc = both[:, :LANES] / both[:, LANES:]
            accs.append(acc[:BLK])
            narrow = acc.astype(BF16)
            for dz in range(1, NZ):
                zs3[dz - 1, :, cols] = narrow[dz * BLK : (dz + 1) * BLK]
        code = head_codes(lses)
        for dz in range(1, NZ):
            zs3[dz - 1, :, INNER:] = code[dz * BLK : (dz + 1) * BLK]

    with jax.named_scope("cross_join"):
        for dz in far_first:
            begin(z_copy(2, zs3, zr3, dz))
        peak = jnp.concatenate([lse[:BLK] for lse in lses], axis=1)
        parts = [(jnp.concatenate(accs, axis=1), peak)]
        for dz in far_first[::-1]:
            z_copy(2, zs3, zr3, dz).wait_recv()
            arrived = zr3[dz - 1]
            parts.append((arrived[:, :INNER].astype(F32), dot(arrived[:, INNER:], spread_heads)))
            peak = jnp.maximum(peak, parts[-1][1])
        weights = [jnp.exp(lse - peak) for _, lse in parts]
        acc, whole = parts[0][0] * weights[0], weights[0]
        for (a, _), w in zip(parts[1:], weights[1:]):
            acc += a * w
            whole += w
        mixed[0] = (acc / whole).astype(BF16)

    with jax.named_scope("cross_out"):
        rows = gather_rows(2, mixed, lambda: cache_end(0))
        inward[4].wait()
        late[3].wait_recv()
        prod[:, :COLS] = dot(rows, wco[...])
        prod[:, COLS:] = dot(rows, far_wco[...])
        head_sums(1, core_s2, core_r2, ys2, yr2, delta2, lambda: cache_start(1))

    with jax.named_scope("pair_columns"):
        last_s[...] = summed[:, COLS:].astype(BF16)
        copy = pair_copy(9, last_s, last_r, pair_peer)
        begin(copy)
        cache_end(1)
        for dz in range(NZ):
            for t in range(2):
                rows = slice(dz * BLK + t * RB, dz * BLK + (t + 1) * RB)
                out[t, rows_at(0, dz), :] = summed[rows, :COLS]
        copy.wait_recv()
        for dz in range(NZ):
            for t in range(2):
                rows = slice(dz * BLK + t * RB, dz * BLK + (t + 1) * RB)
                out[t, rows_at(1, dz), :] = last_r[rows, :].astype(F32)
    for copy in pending:
        copy.wait_send()


def body(
    hidden_in, norm_gains, w_qkv, w_self_out, w_cross_q, w_cross_out, pos_bias, self_cache, memory, parents
):
    dma = pltpu.SemaphoreType.DMA
    wide1, wide2 = 3 * INNER + LANES, INNER + LANES
    half_pair = [pltpu.VMEM((HALF, WIDE), BF16)] * 2
    quarters = [pltpu.VMEM((NY - 1, HALF // NY, WIDE), BF16)] * 2
    head_buffers = [*half_pair, *quarters, pltpu.VMEM((2, NY, HALF // NY, WIDE), BF16)]
    in_vmem = pl.BlockSpec(memory_space=pltpu.VMEM)
    in_hbm = pl.BlockSpec(memory_space=pl.ANY)
    added, cache_rows = pl.pallas_call(
        kernel,
        out_shape=(
            jax.ShapeDtypeStruct(hidden_in.shape, F32),
            jax.ShapeDtypeStruct((2, RB * (PREV + 2), INNER), BF16),
        ),
        in_specs=[in_vmem] * 2 + [in_hbm] * 4 + [in_vmem] * 2 + [in_hbm, in_vmem],
        out_specs=(in_vmem, in_vmem),
        scratch_shapes=[
            pltpu.VMEM((3, COLS, INNER), BF16),
            pltpu.VMEM(w_self_out.shape, BF16),
            pltpu.VMEM(w_cross_q.shape, BF16),
            pltpu.VMEM(w_cross_out.shape, BF16),
            pltpu.VMEM(memory.shape, BF16),
            pltpu.VMEM((ROWS, COLS), F32),
            pltpu.VMEM((ROWS, COLS), F32),
            pltpu.VMEM((8, COLS), F32),
            pltpu.VMEM((8, COLS), F32),
            pltpu.VMEM((3, COLS, INNER), BF16),
            pltpu.VMEM(w_self_out.shape, BF16),
            pltpu.VMEM(w_cross_q.shape, BF16),
            pltpu.VMEM(w_cross_out.shape, BF16),
            pltpu.VMEM(memory.shape, BF16),
            *[pltpu.VMEM((ROWS, WIDE), F32)] * 3,
            *[pltpu.VMEM((NZ - 1, BLK, wide1), BF16)] * 2,
            pltpu.VMEM((ROWS, wide1), F32),
            *[pltpu.VMEM((NZ - 1, BLK, wide2), BF16)] * 2,
            pltpu.VMEM((ROWS, wide2), F32),
            *[pltpu.VMEM((NZ - 1, BLK, wide2), BF16)] * 2,
            *[pltpu.VMEM((NALL, SLOTS * CP, COLS), BF16)] * 2,
            *[pltpu.VMEM((2, NALL, SLOTS * GP, COLS), BF16)] * 2,
            *[pltpu.VMEM((NALL, SLOTS * KP, LANES), BF16)] * 4,
            *[pltpu.VMEM((NZ, BLK, INNER), BF16)] * 3,
            *[pltpu.VMEM((ROWS, COLS), BF16)] * 2,
            *head_buffers,
            *head_buffers,
            dma((10,)), dma((10,)), dma((3, NZ - 1)), dma((3, NZ - 1)),
            dma((NALL,)), dma((NALL,)), dma((2, NALL)), dma((2, NALL)),
            dma((3, NZ)), dma((3, NZ)),
            dma((2,)), dma((2,)), dma((2, NY - 1)), dma((2, NY - 1)),
            dma((2, NY)), dma((2, NY)), dma((2, NY)), dma((2, NY)),
            dma((NALL,)), dma((NALL,)), dma((NALL,)), dma((NALL,)), dma((5,)),
        ],
        compiler_params=pltpu.CompilerParams(
            collective_id=0, has_side_effects=True, vmem_limit_bytes=58 * 1024 * 1024
        ),
        name="decode",
    )(
        hidden_in, norm_gains, w_qkv.transpose(1, 0, 2), w_self_out, w_cross_q, w_cross_out, pos_bias,
        self_cache[:, 0].transpose(0, 2, 1, 3), memory, parents,
    )
    return hidden_in + added, cache_rows.reshape(2, 1, RB, PREV + 2, INNER)


def solution(mesh):
    placed = (
        P(None, "beam", "blk"),
        P(None, "blk"),
        P("blk", None, "head"),
        P("head", "blk"),
        P("blk", "head"),
        P("head", "blk"),
        P("head", None),
        P(None, "beam", "blk", None, "head"),
        P(None, "blk", "head"),
        P(),
    )
    return jax.shard_map(
        body,
        mesh=mesh,
        in_specs=placed,
        out_specs=(P(None, "beam", "blk"), P(None, "beam", "blk", None, "head")),
        check_vma=False,
    )
```
